32 devices in a mesh: grp: 2 (over x), ctx: 8 (over z, y), head: 2 (over core).
Axes of the slice: x: 2, y: 2, z: 4, core: 2. Of those that a mesh axis runs over, the one named last changes fastest.
Arguments:
- queries: bfloat16 [3072, 16, 128], P(('grp', 'ctx'), 'head'), parts along dimension 0
- key_vecs: bfloat16 [3072, 16, 128], P(('grp', 'ctx'), 'head'), parts along dimension 0
- value_vecs: bfloat16 [3072, 16, 128], P(('grp', 'ctx'), 'head'), parts along dimension 0, may hold values from -6 to 6
- out_grad: bfloat16 [3072, 16, 128], P(('grp', 'ctx'), 'head'), parts along dimension 0, may hold values from -6 to 6
- doc_ids: int32 [3072], P('grp'), parts along dimension 0, may hold values from 0 to 5, never falling along the last dimension, each value on 1 to 960 neighbouring positions
Outputs:
- attn_out: bfloat16 [3072, 16, 128], P(('grp', 'ctx'), 'head'), parts along dimension 0
- query_grad: bfloat16 [3072, 16, 128], P(('grp', 'ctx'), 'head'), parts along dimension 0
- key_grad: bfloat16 [3072, 16, 128], P(('grp', 'ctx'), 'head'), parts along dimension 0
- value_grad: bfloat16 [3072, 16, 128], P(('grp', 'ctx'), 'head'), parts along dimension 0
The draws below stay inside these ranges and needn't reach their ends.
There are 2 independent parts, one for each index of `grp`. The reference program is written for one: setup_inputs(seed, part) draws one part's arguments, and reference() takes and returns one part's arrays. A program takes and returns all parts, laid end to end along the dimension named above; each array names one. Nothing has to cross between parts.
Inputs may be any that keep to these rules, and one draw needn't show every extreme that they name: doc_ids never fall along the sequence; every document has 1 to 960 tokens and one has exactly 960.
All inputs are finite; a program needn't handle non-finite values.
Results may differ from the reference program's by a relative error of at most 0.035.
Values may be sent and summed in bfloat16 or wider, within the bound.
A program may use at most 128 MiB of HBM per device.

```python
import math
import jax
import jax.numpy as jnp
import numpy as np
from jax import lax

DH = 128
HEADS = 16
S_DEV = 192
DOCS = 6
TOKENS = 1536
DOC_MOST = 960
N_CTX = 8


def paired_vectors(key):
    base = jax.random.fold_in(key, 7)
    key_query, key_key = jax.random.split(base, 2)
    shape = (TOKENS, HEADS, DH)
    query_vals = jnp.clip(jax.random.normal(key_query, shape, jnp.float32), -6.0, 6.0)
    key_vals = jnp.clip(jax.random.normal(key_key, shape, jnp.float32), -6.0, 6.0)
    return (query_vals, key_vals)


def draw_queries(key, part):
    return paired_vectors(key)[0].astype(jnp.bfloat16)


def draw_key_vecs(key, part):
    return paired_vectors(key)[1].astype(jnp.bfloat16)


def block_scale(key, dims, pieces, low, top_value):
    factor_of = 1.0
    for dim, parts in pieces:
        draws = jax.random.uniform(jax.random.fold_in(jax.random.fold_in(key, 6), dim), (parts,), jnp.float32, low / len(pieces), top_value / len(pieces))
        factor_of = factor_of * jnp.repeat(jnp.exp(draws), dims[dim] // parts).reshape((-1,) + (1,) * (len(dims) - 1 - dim))
    return factor_of


def profile(count, total, limit, slope):
    weights = [(1 << 20) // math.isqrt(rank ** slope) + 1 for rank in range(2, count + 1)]
    spare, given = total - limit - (count - 1), [1] * (count - 1)
    while spare > 0:
        movable = [i for i in range(count - 1) if given[i] < limit]
        pool, budget = sum([weights[i] for i in movable]), spare
        for i in movable:
            more = min(limit - given[i], max(1, budget * weights[i] // pool), spare)
            given[i] = given[i] + more
            spare = spare - more
    return np.array([limit] + given)


def uneven(stream_key, number_of, total, limit, slope):
    if number_of == 2:
        one = jax.random.randint(stream_key, (), max(1, total - limit), min(limit, total - 1) + 1)
        return jnp.stack([one, total - one])
    sizes = jnp.asarray(profile(number_of, total, limit, slope), jnp.int32)
    couples = (number_of - 1) // 2
    giver, taker = sizes[1:1 + 2 * couples:2], sizes[2:2 + 2 * couples:2]
    room = jnp.minimum(giver - 1, limit - taker)
    moved = jax.random.randint(jax.random.fold_in(stream_key, 1), (couples,), 0, 1 << 20) % (room + 1)
    sizes = sizes.at[1:1 + 2 * couples:2].set(giver - moved).at[2:2 + 2 * couples:2].set(taker + moved)
    return sizes[jax.random.permutation(jax.random.fold_in(stream_key, 2), number_of)]


def scatter_about(own_key, shape, spread, bound, pieces=(), held_as=jnp.bfloat16):
    values = jax.random.normal(own_key, shape, jnp.float32) * spread
    if len(pieces) > 0:
        values = block_scale(own_key, shape, pieces, -0.22, 0.18) * values
    return jnp.clip(values, min=-bound, max=bound).astype(held_as)


def setup_inputs(seed: int = 0, part: int = 0) -> dict:
    key_of = jax.random.split(jax.random.key(seed), 6)
    part_splits = jax.random.split(jax.random.fold_in(key_of[5], part), 6)
    return {
        "queries": draw_queries(jax.random.fold_in(jax.random.fold_in(key_of[5], part), 71), part),
        "key_vecs": draw_key_vecs(jax.random.fold_in(jax.random.fold_in(key_of[5], part), 71), part),
        "value_vecs": scatter_about(part_splits[2], (TOKENS, HEADS, DH), 1.0, 6.0, ((0, 8), (1, 2))),
        "out_grad": scatter_about(part_splits[3], (TOKENS, HEADS, DH), 1.0, 6.0, ((0, 8), (1, 2))),
        "doc_ids": jnp.searchsorted(jnp.cumsum(uneven(part_splits[4], DOCS, TOKENS, DOC_MOST, 2)), jnp.arange(TOKENS), side="right").astype(jnp.int32),
    }


def one_head(operands, visible):
    query_rows, key_rows, value_rows, grad_rows = operands
    scaling = DH ** -0.5
    scores = jnp.dot(query_rows, key_rows.T, preferred_element_type=jnp.float32) * scaling
    largest = jnp.max(jnp.where(visible, scores, -1e30), axis=-1)
    weights = jnp.where(visible, jnp.exp(scores - largest[:, None]), 0.0)
    lse = largest + jnp.log(jnp.sum(weights, axis=-1))
    probs = jnp.where(visible, jnp.exp(scores - lse[:, None]), 0.0).astype(jnp.bfloat16)
    attn_out = jnp.dot(probs, value_rows, preferred_element_type=jnp.float32).astype(jnp.bfloat16)
    delta = jnp.sum(grad_rows.astype(jnp.float32) * attn_out.astype(jnp.float32), axis=-1)
    dprobs = jnp.dot(grad_rows, value_rows.T, preferred_element_type=jnp.float32)
    dscores = (probs.astype(jnp.float32) * (dprobs - delta[:, None])).astype(jnp.bfloat16)
    query_grad = (scaling * jnp.dot(dscores, key_rows, preferred_element_type=jnp.float32)).astype(jnp.bfloat16)
    key_grad = (scaling * jnp.dot(dscores.T, query_rows, preferred_element_type=jnp.float32)).astype(jnp.bfloat16)
    value_grad = jnp.dot(probs.T, grad_rows, preferred_element_type=jnp.float32).astype(jnp.bfloat16)
    return attn_out, query_grad, key_grad, value_grad


def stored_position(rows, shard_rows, shard_count):
    half_rows = shard_rows // 2
    shard = rows // shard_rows
    within = rows % shard_rows
    return jnp.where(within < half_rows, shard * half_rows + within,
                     (2 * shard_count - 1 - shard) * half_rows + within - half_rows).astype(jnp.int32)


def reference(queries, key_vecs, value_vecs, out_grad, doc_ids):
    rows = jnp.arange(TOKENS, dtype=jnp.int32)
    position = stored_position(rows, S_DEV, N_CTX)
    row_doc = jnp.take(doc_ids, position)
    visible = (row_doc[None, :] == row_doc[:, None]) & (position[None, :] <= position[:, None])
    stacked = tuple(jnp.transpose(array, (1, 0, 2)) for array in (queries, key_vecs, value_vecs, out_grad))
    results = lax.map(lambda operands: one_head(operands, visible), stacked)
    attn_out, query_grad, key_grad, value_grad = tuple(jnp.transpose(array, (1, 0, 2)) for array in results)
    return (attn_out, query_grad, key_grad, value_grad)
```

```python
import functools

import jax
import jax.numpy as jnp
from jax import lax
from jax.experimental import pallas as pl
from jax.experimental.pallas import tpu as pltpu
from jax.sharding import PartitionSpec as P


def block_length(shard_rows, shard_count):
    factor = 1
    while factor * shard_rows < 512 and shard_count % (factor * 2) == 0:
        factor = factor * 2
    return factor * shard_rows


def stored_position(rows, shard_rows, shard_count):
    half_rows = shard_rows // 2
    shard = rows // shard_rows
    within = rows % shard_rows
    return jnp.where(
        within < half_rows,
        shard * half_rows + within,
        (2 * shard_count - 1 - shard) * half_rows + within - half_rows,
    )


def score_block(query_blk, query_pos, query_doc, key_blk, key_pos, key_doc, scaling):
    scores = (
        jnp.einsum("qhd,khd->hqk", query_blk, key_blk, preferred_element_type=jnp.float32) * scaling
    )
    allowed = (key_doc[None, :] == query_doc[:, None]) & (key_pos[None, :] <= query_pos[:, None])
    return (scores, allowed[None])


def probs_of(scores, allowed, lse):
    return jnp.where(allowed, jnp.exp(scores - lse[:, :, None]), 0.0).astype(jnp.bfloat16)


def dscores_of(probs, grad_blk, value_blk, delta):
    dprobs = jnp.einsum("qhd,khd->hqk", grad_blk, value_blk, preferred_element_type=jnp.float32)
    return (probs.astype(jnp.float32) * (dprobs - delta[:, :, None])).astype(jnp.bfloat16)


def gathered(queries, key_vecs, value_vecs, out_grad, doc_ids):
    shard_rows = queries.shape[0]
    head_count = queries.shape[1]
    head_size = queries.shape[2]
    scaling = head_size ** (-0.5)
    shard_count = lax.axis_size("ctx")
    shard_index = lax.axis_index("ctx")
    own_start = shard_index * shard_rows

    def positions(start, length):
        return stored_position(start + jnp.arange(length, dtype=jnp.int32), shard_rows, shard_count)

    own_pos = positions(own_start, shard_rows)
    own_doc = jnp.take(doc_ids, own_pos)
    keys_all, values_all = (
        lax.all_gather(key_vecs, "ctx", axis=0, tiled=True),
        lax.all_gather(value_vecs, "ctx", axis=0, tiled=True),
    )
    block = block_length(shard_rows, shard_count)
    block_count = keys_all.shape[0] // block

    def key_slices(start, length):
        key_blk = lax.dynamic_slice_in_dim(keys_all, start, length, 0)
        value_blk = lax.dynamic_slice_in_dim(values_all, start, length, 0)
        key_pos = positions(start, length)
        key_doc = jnp.take(doc_ids, key_pos)
        return (key_blk, value_blk, key_pos, key_doc)

    def stat_step(index, carry):
        running, total = carry
        key_blk, value_blk, key_pos, key_doc = key_slices(index * block, block)
        scores, allowed = score_block(queries, own_pos, own_doc, key_blk, key_pos, key_doc, scaling)
        newmax = jnp.maximum(running, jnp.max(jnp.where(allowed, scores, -1e30), axis=-1))
        total = total * jnp.exp(running - newmax) + jnp.sum(
            jnp.where(allowed, jnp.exp(scores - newmax[:, :, None]), 0.0), axis=-1
        )
        return (newmax, total)

    start_max = jnp.full((head_count, shard_rows), -1e30, jnp.float32)
    start_sum = jnp.zeros((head_count, shard_rows), jnp.float32)
    running, total = lax.fori_loop(0, block_count, stat_step, (start_max, start_sum))
    lse = running + jnp.log(total)

    def out_step(index, accum):
        key_blk, value_blk, key_pos, key_doc = key_slices(index * block, block)
        scores, allowed = score_block(queries, own_pos, own_doc, key_blk, key_pos, key_doc, scaling)
        probs = probs_of(scores, allowed, lse)
        return accum + jnp.einsum(
            "hqk,khd->qhd", probs, value_blk, preferred_element_type=jnp.float32
        )

    zero_rows = jnp.zeros((shard_rows, head_count, head_size), jnp.float32)
    attn_out = lax.fori_loop(0, block_count, out_step, zero_rows).astype(jnp.bfloat16)
    delta_rows = jnp.sum(out_grad.astype(jnp.float32) * attn_out.astype(jnp.float32), axis=-1)
    delta = delta_rows.T

    def query_step(index, accum):
        key_blk, value_blk, key_pos, key_doc = key_slices(index * block, block)
        scores, allowed = score_block(queries, own_pos, own_doc, key_blk, key_pos, key_doc, scaling)
        probs = probs_of(scores, allowed, lse)
        dscores = dscores_of(probs, out_grad, value_blk, delta)
        return accum + jnp.einsum(
            "hqk,khd->qhd", dscores, key_blk, preferred_element_type=jnp.float32
        )

    query_grad = (scaling * lax.fori_loop(0, block_count, query_step, zero_rows)).astype(
        jnp.bfloat16
    )
    lse_all, delta_all = (
        lax.all_gather(lse.T, "ctx", axis=0, tiled=True),
        lax.all_gather(delta_rows, "ctx", axis=0, tiled=True),
    )
    query_blk = lax.all_gather(queries, "ctx", axis=0, tiled=True)
    grad_blk = lax.all_gather(out_grad, "ctx", axis=0, tiled=True)
    length = query_blk.shape[0]
    query_pos = positions(jnp.int32(0), length)
    query_doc = jnp.take(doc_ids, query_pos)
    lse_blk = lse_all.T
    delta_blk = delta_all.T
    scores, allowed = score_block(
        query_blk, query_pos, query_doc, key_vecs, own_pos, own_doc, scaling
    )
    probs = probs_of(scores, allowed, lse_blk)
    dscores = dscores_of(probs, grad_blk, value_vecs, delta_blk)
    key_accum = scaling * jnp.einsum(
        "hqk,qhd->khd", dscores, query_blk, preferred_element_type=jnp.float32
    )
    value_accum = jnp.einsum("hqk,qhd->khd", probs, grad_blk, preferred_element_type=jnp.float32)
    key_grad = key_accum.astype(jnp.bfloat16)
    value_grad = value_accum.astype(jnp.bfloat16)
    return (attn_out, query_grad, key_grad, value_grad)


KEY, QUERY, VALUE, GRAD = 0, 1, 2, 3
OUT, DQ, DK, DV = 0, 1, 2, 3
LOG2E = 1.4426950408889634


def nt_dot(a, b):
    return lax.dot_general(a, b, (((1,), (1,)), ((), ())), preferred_element_type=jnp.float32)


def head_kernel(
    shards,
    half,
    group,
    key_ref,
    query_ref,
    value_ref,
    grad_ref,
    doc_ref,
    out_ref,
    staged,
    wide,
    full,
    ready,
    doc_col,
    key_t,
    value_t,
    out_t,
    score_buf,
    prob_buf,
    key_acc,
    value_acc,
    in_send,
    in_recv,
    out_send,
    out_recv,
):
    me = lax.axis_index("ctx")
    size = half * group
    blocks = 2 * shards // group
    head_size = full.shape[-1]
    scaling = head_size ** (-0.5)

    barrier = pltpu.get_barrier_semaphore()

    def greet(step, carry):
        pl.semaphore_signal(
            barrier,
            inc=1,
            device_id={"ctx": lax.rem(me + step, shards)},
            device_id_type=pl.DeviceIdType.MESH,
        )
        return carry

    lax.fori_loop(1, shards, greet, 0)

    def stage(kind, ref):
        rows = ref.shape[0]
        wide[...] = ref[...].astype(jnp.float32).reshape(rows * shards, head_size)
        for head in range(shards):
            staged[kind, head] = wide[pl.ds(head, rows, stride=shards), :].astype(jnp.bfloat16)

    def part_rows(part):
        return pl.ds(part * half, half)

    def block_rows(index):
        return pl.ds(pl.multiple_of(index * half, half), half)

    def position(part):
        return me if part == 0 else 2 * shards - 1 - me

    def send_in(kind, part):
        where = position(part)
        pltpu.make_async_copy(
            staged.at[kind, me, part_rows(part)],
            full.at[kind, block_rows(where)],
            in_recv.at[kind, where],
        ).start()

        def one(step, carry):
            target = lax.rem(me + step, shards)
            pltpu.make_async_remote_copy(
                src_ref=staged.at[kind, target, part_rows(part)],
                dst_ref=full.at[kind, block_rows(where)],
                send_sem=in_send.at[kind, part, step],
                recv_sem=in_recv.at[kind, where],
                device_id={"ctx": target},
                device_id_type=pl.DeviceIdType.MESH,
            ).start()
            return carry

        lax.fori_loop(1, shards, one, 0)

    def wait_in(kind, block):
        def one(index, carry):
            held = full.at[kind, block_rows(index)]
            pltpu.make_async_copy(held, held, in_recv.at[kind, index]).wait()
            return carry

        lax.fori_loop(block * group, (block + 1) * group, one, 0)

    def send_out(kind, block):
        for index in range(block * group, (block + 1) * group):
            part = 0 if index < shards else 1
            owner = index if part == 0 else 2 * shards - 1 - index
            held = ready.at[kind, pl.ds(index * half, half)]
            place = out_ref.at[kind, me, part_rows(part)]

            @pl.when(owner == me)
            def _():
                pltpu.make_async_copy(held, place, out_recv.at[kind, part, me]).start()

            @pl.when(owner != me)
            def _():
                pltpu.make_async_remote_copy(
                    src_ref=held,
                    dst_ref=place,
                    send_sem=out_send.at[kind, index],
                    recv_sem=out_recv.at[kind, part, me],
                    device_id={"ctx": owner},
                    device_id_type=pl.DeviceIdType.MESH,
                ).start()

    stage(KEY, key_ref)
    stage(QUERY, query_ref)
    pl.semaphore_wait(barrier, shards - 1)
    send_in(KEY, 0)
    send_in(QUERY, 0)
    stage(VALUE, value_ref)
    send_in(VALUE, 0)
    send_in(KEY, 1)
    send_in(QUERY, 1)
    send_in(VALUE, 1)
    stage(GRAD, grad_ref)
    send_in(GRAD, 1)
    send_in(GRAD, 0)

    docs = doc_ref[...].astype(jnp.float32)
    for block in range(blocks):
        piece = docs[:, block * size : (block + 1) * size]
        doc_col[block] = jnp.broadcast_to(piece, (128, size)).T

    def rows_of(block):
        return pl.ds(block * size, size)

    for block in range(blocks):
        wait_in(KEY, block)
        wait_in(QUERY, block)
        queries = full[QUERY, rows_of(block)]
        query_doc = docs[:, block * size : (block + 1) * size]
        largest = None
        for other in range(block + 1):
            scores = nt_dot(full[KEY, rows_of(other)], queries)
            key_doc = jnp.concatenate([doc_col[other]] * (size // 128), axis=1)
            seen = key_doc == query_doc
            if other == block:
                key_at = lax.broadcasted_iota(jnp.int32, (size, size), 0)
                query_at = lax.broadcasted_iota(jnp.int32, (size, size), 1)
                seen = seen & (key_at <= query_at)
            scores = jnp.where(seen, scores, -1e30)
            score_buf[other] = scores
            top = jnp.max(scores, axis=0, keepdims=True)
            largest = top if largest is None else jnp.maximum(largest, top)
        total = jnp.zeros((1, size), jnp.float32)
        for other in range(block + 1):
            weights = jnp.exp2((score_buf[other] - largest) * (scaling * LOG2E))
            score_buf[other] = weights
            total = total + jnp.sum(weights, axis=0, keepdims=True)
        inverse = 1.0 / total
        wait_in(VALUE, block)
        value_t[block] = full[VALUE, rows_of(block)].astype(jnp.float32).T.astype(jnp.bfloat16)
        key_t[block] = full[KEY, rows_of(block)].astype(jnp.float32).T.astype(jnp.bfloat16)
        accum = jnp.zeros((head_size, size), jnp.float32)
        for other in range(block + 1):
            probs = (score_buf[other] * inverse).astype(jnp.bfloat16)
            prob_buf[block, other] = probs
            accum = accum + jnp.dot(value_t[other], probs, preferred_element_type=jnp.float32)
        rounded = accum.astype(jnp.bfloat16).astype(jnp.float32)
        out_t[block] = rounded
        ready[OUT, rows_of(block)] = rounded.T.astype(jnp.bfloat16)
        send_out(OUT, block)

    for block in reversed(range(blocks)):
        wait_in(GRAD, block)
        queries = full[QUERY, rows_of(block)]
        grads = full[GRAD, rows_of(block)]
        delta = jnp.sum(grads.astype(jnp.float32).T * out_t[block], axis=0, keepdims=True)
        accum = jnp.zeros((head_size, size), jnp.float32)
        for other in range(block + 1):
            probs = prob_buf[block, other]
            dprobs = nt_dot(full[VALUE, rows_of(other)], grads)
            dscores = (probs.astype(jnp.float32) * (dprobs - delta)).astype(jnp.bfloat16)
            value_part = jnp.dot(probs, grads, preferred_element_type=jnp.float32)
            key_part = jnp.dot(dscores, queries, preferred_element_type=jnp.float32)
            if block < blocks - 1:
                value_part = value_part + value_acc[other]
                key_part = key_part + key_acc[other]
            if other < block:
                value_acc[other] = value_part
                key_acc[other] = key_part
            else:
                ready[DV, rows_of(block)] = value_part.astype(jnp.bfloat16)
                ready[DK, rows_of(block)] = (scaling * key_part).astype(jnp.bfloat16)
            accum = accum + jnp.dot(key_t[other], dscores, preferred_element_type=jnp.float32)
        ready[DQ, rows_of(block)] = (scaling * accum).T.astype(jnp.bfloat16)
        for kind in (DV, DK, DQ):
            send_out(kind, block)

    def drain(step, carry):
        target = lax.rem(me + step, shards)
        for kind in range(4):
            for part in range(2):
                left = staged.at[kind, target, part_rows(part)]
                pltpu.make_async_copy(left, left, in_send.at[kind, part, step]).wait()
        return carry

    lax.fori_loop(1, shards, drain, 0)

    def drain_out(index, carry):
        owner = jnp.where(index < shards, index, 2 * shards - 1 - index)

        @pl.when(owner != me)
        def _():
            for kind in range(4):
                left = ready.at[kind, block_rows(index)]
                pltpu.make_async_copy(left, left, out_send.at[kind, index]).wait()

        return carry

    lax.fori_loop(0, 2 * shards, drain_out, 0)

    def collect(source, carry):
        for kind in range(4):
            for part in range(2):
                place = out_ref.at[kind, source, part_rows(part)]
                pltpu.make_async_copy(place, place, out_recv.at[kind, part, source]).wait()
        return carry

    lax.fori_loop(0, shards, collect, 0)


def by_heads(queries, key_vecs, value_vecs, out_grad, doc_ids):
    shard_rows, head_count, head_size = queries.shape
    shards = lax.axis_size("ctx")
    half = shard_rows // 2
    tokens = shard_rows * shards
    group = 4
    size = group * half
    blocks = tokens // size
    bf16, f32 = jnp.bfloat16, jnp.float32
    vmem = pl.BlockSpec(memory_space=pltpu.VMEM)
    flops = 7 * tokens * tokens * head_size
    results = pl.pallas_call(
        functools.partial(head_kernel, shards, half, group),
        out_shape=jax.ShapeDtypeStruct((4, shards, shard_rows, head_size), bf16),
        in_specs=[vmem] * 5,
        out_specs=pl.BlockSpec(memory_space=pl.ANY),
        scratch_shapes=[
            pltpu.VMEM((4, shards, shard_rows, head_size), bf16),
            pltpu.VMEM((tokens, head_size), f32),
            pltpu.VMEM((4, tokens, head_size), bf16),
            pltpu.VMEM((4, tokens, head_size), bf16),
            pltpu.VMEM((blocks, size, 128), f32),
            pltpu.VMEM((blocks, head_size, size), bf16),
            pltpu.VMEM((blocks, head_size, size), bf16),
            pltpu.VMEM((blocks, head_size, size), f32),
            pltpu.VMEM((blocks, size, size), f32),
            pltpu.VMEM((blocks, blocks, size, size), bf16),
            pltpu.VMEM((blocks, size, head_size), f32),
            pltpu.VMEM((blocks, size, head_size), f32),
            pltpu.SemaphoreType.DMA((4, 2, shards)),
            pltpu.SemaphoreType.DMA((4, 2 * shards)),
            pltpu.SemaphoreType.DMA((4, 2 * shards)),
            pltpu.SemaphoreType.DMA((4, 2, shards)),
        ],
        compiler_params=pltpu.CompilerParams(
            collective_id=0, has_side_effects=True, vmem_limit_bytes=40 * 1024 * 1024
        ),
        cost_estimate=pl.CostEstimate(
            flops=flops, bytes_accessed=8 * queries.size * 2, transcendentals=tokens * tokens // 2
        ),
    )(key_vecs, queries, value_vecs, out_grad, doc_ids.reshape(1, tokens))
    return tuple(jnp.swapaxes(results[kind], 0, 1) for kind in range(4))


def on_device(queries, key_vecs, value_vecs, out_grad, doc_ids):
    shard_rows, head_count, head_size = queries.shape
    fits = (
        head_count == lax.axis_size("ctx")
        and shard_rows % 32 == 0
        and (2 * shard_rows) % 128 == 0
        and head_size == 128
    )
    attend = by_heads if fits else gathered
    return attend(queries, key_vecs, value_vecs, out_grad, doc_ids)


def solution(mesh):
    return jax.shard_map(
        on_device,
        mesh=mesh,
        in_specs=(
            P(("grp", "ctx"), "head", None),
            P(("grp", "ctx"), "head", None),
            P(("grp", "ctx"), "head", None),
            P(("grp", "ctx"), "head", None),
            P("grp"),
        ),
        out_specs=(
            P(("grp", "ctx"), "head", None),
            P(("grp", "ctx"), "head", None),
            P(("grp", "ctx"), "head", None),
            P(("grp", "ctx"), "head", None),
        ),
        check_vma=False,
    )
```

```python
import functools

import jax
import jax.numpy as jnp
from jax import lax
from jax.experimental import pallas as pl
from jax.experimental.pallas import tpu as pltpu
from jax.sharding import PartitionSpec as P


def block_length(shard_rows, shard_count):
    factor = 1
    while factor * shard_rows < 512 and shard_count % (factor * 2) == 0:
        factor = factor * 2
    return factor * shard_rows


def stored_position(rows, shard_rows, shard_count):
    half_rows = shard_rows // 2
    shard = rows // shard_rows
    within = rows % shard_rows
    return jnp.where(
        within < half_rows,
        shard * half_rows + within,
        (2 * shard_count - 1 - shard) * half_rows + within - half_rows,
    )


def score_block(query_blk, query_pos, query_doc, key_blk, key_pos, key_doc, scaling):
    scores = (
        jnp.einsum("qhd,khd->hqk", query_blk, key_blk, preferred_element_type=jnp.float32) * scaling
    )
    allowed = (key_doc[None, :] == query_doc[:, None]) & (key_pos[None, :] <= query_pos[:, None])
    return (scores, allowed[None])


def probs_of(scores, allowed, lse):
    return jnp.where(allowed, jnp.exp(scores - lse[:, :, None]), 0.0).astype(jnp.bfloat16)


def dscores_of(probs, grad_blk, value_blk, delta):
    dprobs = jnp.einsum("qhd,khd->hqk", grad_blk, value_blk, preferred_element_type=jnp.float32)
    return (probs.astype(jnp.float32) * (dprobs - delta[:, :, None])).astype(jnp.bfloat16)


def gathered(queries, key_vecs, value_vecs, out_grad, doc_ids):
    shard_rows = queries.shape[0]
    head_count = queries.shape[1]
    head_size = queries.shape[2]
    scaling = head_size ** (-0.5)
    shard_count = lax.axis_size("ctx")
    shard_index = lax.axis_index("ctx")
    own_start = shard_index * shard_rows

    def positions(start, length):
        return stored_position(start + jnp.arange(length, dtype=jnp.int32), shard_rows, shard_count)

    own_pos = positions(own_start, shard_rows)
    own_doc = jnp.take(doc_ids, own_pos)
    keys_all, values_all = (
        lax.all_gather(key_vecs, "ctx", axis=0, tiled=True),
        lax.all_gather(value_vecs, "ctx", axis=0, tiled=True),
    )
    block = block_length(shard_rows, shard_count)
    block_count = keys_all.shape[0] // block

    def key_slices(start, length):
        key_blk = lax.dynamic_slice_in_dim(keys_all, start, length, 0)
        value_blk = lax.dynamic_slice_in_dim(values_all, start, length, 0)
        key_pos = positions(start, length)
        key_doc = jnp.take(doc_ids, key_pos)
        return (key_blk, value_blk, key_pos, key_doc)

    def stat_step(index, carry):
        running, total = carry
        key_blk, value_blk, key_pos, key_doc = key_slices(index * block, block)
        scores, allowed = score_block(queries, own_pos, own_doc, key_blk, key_pos, key_doc, scaling)
        newmax = jnp.maximum(running, jnp.max(jnp.where(allowed, scores, -1e30), axis=-1))
        total = total * jnp.exp(running - newmax) + jnp.sum(
            jnp.where(allowed, jnp.exp(scores - newmax[:, :, None]), 0.0), axis=-1
        )
        return (newmax, total)

    start_max = jnp.full((head_count, shard_rows), -1e30, jnp.float32)
    start_sum = jnp.zeros((head_count, shard_rows), jnp.float32)
    running, total = lax.fori_loop(0, block_count, stat_step, (start_max, start_sum))
    lse = running + jnp.log(total)

    def out_step(index, accum):
        key_blk, value_blk, key_pos, key_doc = key_slices(index * block, block)
        scores, allowed = score_block(queries, own_pos, own_doc, key_blk, key_pos, key_doc, scaling)
        probs = probs_of(scores, allowed, lse)
        return accum + jnp.einsum(
            "hqk,khd->qhd", probs, value_blk, preferred_element_type=jnp.float32
        )

    zero_rows = jnp.zeros((shard_rows, head_count, head_size), jnp.float32)
    attn_out = lax.fori_loop(0, block_count, out_step, zero_rows).astype(jnp.bfloat16)
    delta_rows = jnp.sum(out_grad.astype(jnp.float32) * attn_out.astype(jnp.float32), axis=-1)
    delta = delta_rows.T

    def query_step(index, accum):
        key_blk, value_blk, key_pos, key_doc = key_slices(index * block, block)
        scores, allowed = score_block(queries, own_pos, own_doc, key_blk, key_pos, key_doc, scaling)
        probs = probs_of(scores, allowed, lse)
        dscores = dscores_of(probs, out_grad, value_blk, delta)
        return accum + jnp.einsum(
            "hqk,khd->qhd", dscores, key_blk, preferred_element_type=jnp.float32
        )

    query_grad = (scaling * lax.fori_loop(0, block_count, query_step, zero_rows)).astype(
        jnp.bfloat16
    )
    lse_all, delta_all = (
        lax.all_gather(lse.T, "ctx", axis=0, tiled=True),
        lax.all_gather(delta_rows, "ctx", axis=0, tiled=True),
    )
    query_blk = lax.all_gather(queries, "ctx", axis=0, tiled=True)
    grad_blk = lax.all_gather(out_grad, "ctx", axis=0, tiled=True)
    length = query_blk.shape[0]
    query_pos = positions(jnp.int32(0), length)
    query_doc = jnp.take(doc_ids, query_pos)
    lse_blk = lse_all.T
    delta_blk = delta_all.T
    scores, allowed = score_block(
        query_blk, query_pos, query_doc, key_vecs, own_pos, own_doc, scaling
    )
    probs = probs_of(scores, allowed, lse_blk)
    dscores = dscores_of(probs, grad_blk, value_vecs, delta_blk)
    key_accum = scaling * jnp.einsum(
        "hqk,qhd->khd", dscores, query_blk, preferred_element_type=jnp.float32
    )
    value_accum = jnp.einsum("hqk,qhd->khd", probs, grad_blk, preferred_element_type=jnp.float32)
    key_grad = key_accum.astype(jnp.bfloat16)
    value_grad = value_accum.astype(jnp.bfloat16)
    return (attn_out, query_grad, key_grad, value_grad)


KEY, QUERY, VALUE, GRAD = 0, 1, 2, 3
OUT, DQ, DK, DV = 0, 1, 2, 3
LOG2E = 1.4426950408889634


def nt_dot(a, b):
    return lax.dot_general(a, b, (((1,), (1,)), ((), ())), preferred_element_type=jnp.float32)


def head_kernel(
    shards,
    half,
    group,
    key_ref,
    query_ref,
    value_ref,
    grad_ref,
    doc_ref,
    out_ref,
    fetched,
    staged,
    wide,
    full,
    ready,
    doc_col,
    key_t,
    value_t,
    out_t,
    score_buf,
    prob_buf,
    key_acc,
    value_acc,
    in_send,
    in_recv,
    out_send,
    out_recv,
    fetch_sem,
):
    me = lax.axis_index("ctx")
    size = half * group
    blocks = 2 * shards // group
    head_size = full.shape[-1]
    scaling = head_size ** (-0.5)

    fetches = [
        pltpu.make_async_copy(ref, fetched.at[kind], fetch_sem.at[kind])
        for kind, ref in ((KEY, key_ref), (QUERY, query_ref), (VALUE, value_ref), (GRAD, grad_ref))
    ]
    for fetch in fetches:
        fetch.start()

    barrier = pltpu.get_barrier_semaphore()

    def greet(step, carry):
        pl.semaphore_signal(
            barrier,
            inc=1,
            device_id={"ctx": lax.rem(me + step, shards)},
            device_id_type=pl.DeviceIdType.MESH,
        )
        return carry

    lax.fori_loop(1, shards, greet, 0)

    def stage(kind):
        fetches[kind].wait()
        rows = fetched.shape[1]
        wide[...] = fetched[kind].astype(jnp.float32).reshape(rows * shards, head_size)
        for head in range(shards):
            staged[kind, head] = wide[pl.ds(head, rows, stride=shards), :].astype(jnp.bfloat16)

    def part_rows(part):
        return pl.ds(part * half, half)

    def block_rows(index):
        return pl.ds(pl.multiple_of(index * half, half), half)

    def position(part):
        return me if part == 0 else 2 * shards - 1 - me

    def far_first(step):
        return lax.rem(step + shards // 2 - 2, shards - 1) + 1

    def sent_in(kind, part):
        def one(step, carry):
            left = staged.at[kind, lax.rem(me + far_first(step), shards), part_rows(part)]
            pltpu.make_async_copy(left, left, in_send.at[kind, part, step]).wait()
            return carry

        lax.fori_loop(1, shards, one, 0)

    def send_in(kind, part):
        where = position(part)
        pltpu.make_async_copy(
            staged.at[kind, me, part_rows(part)],
            full.at[kind, block_rows(where)],
            in_recv.at[kind, where],
        ).start()

        def one(step, carry):
            target = lax.rem(me + far_first(step), shards)
            pltpu.make_async_remote_copy(
                src_ref=staged.at[kind, target, part_rows(part)],
                dst_ref=full.at[kind, block_rows(where)],
                send_sem=in_send.at[kind, part, step],
                recv_sem=in_recv.at[kind, where],
                device_id={"ctx": target},
                device_id_type=pl.DeviceIdType.MESH,
            ).start()
            return carry

        lax.fori_loop(1, shards, one, 0)

    def wait_in(kind, block):
        def one(index, carry):
            held = full.at[kind, block_rows(index)]
            pltpu.make_async_copy(held, held, in_recv.at[kind, index]).wait()
            return carry

        lax.fori_loop(block * group, (block + 1) * group, one, 0)

    def send_out(kind, block):
        for index in range(block * group, (block + 1) * group):
            part = 0 if index < shards else 1
            owner = index if part == 0 else 2 * shards - 1 - index
            held = ready.at[kind, pl.ds(index * half, half)]
            place = out_ref.at[kind, me, part_rows(part)]

            @pl.when(owner == me)
            def _():
                pltpu.make_async_copy(held, place, out_recv.at[kind, part, me]).start()

            @pl.when(owner != me)
            def _():
                pltpu.make_async_remote_copy(
                    src_ref=held,
                    dst_ref=place,
                    send_sem=out_send.at[kind, index],
                    recv_sem=out_recv.at[kind, part, me],
                    device_id={"ctx": owner},
                    device_id_type=pl.DeviceIdType.MESH,
                ).start()

    stage(KEY)
    pl.semaphore_wait(barrier, shards - 1)
    send_in(KEY, 0)
    stage(QUERY)
    send_in(QUERY, 0)
    stage(VALUE)
    send_in(VALUE, 0)
    stage(GRAD)

    docs = doc_ref[...].astype(jnp.float32).reshape(1, -1)
    for block in range(blocks):
        piece = docs[:, block * size : (block + 1) * size]
        doc_col[block] = jnp.broadcast_to(piece, (128, size)).T

    for kind in (KEY, QUERY, VALUE):
        sent_in(kind, 0)
        send_in(kind, 1)

    def rows_of(block):
        return pl.ds(block * size, size)

    for block in range(blocks):
        if block == blocks // 2:
            for kind, part in ((KEY, 1), (QUERY, 0)):
                sent_in(kind, 1)
                send_in(GRAD, part)
        wait_in(KEY, block)
        wait_in(QUERY, block)
        queries = full[QUERY, rows_of(block)]
        query_doc = docs[:, block * size : (block + 1) * size]
        largest = None
        for other in range(block + 1):
            scores = nt_dot(full[KEY, rows_of(other)], queries)
            key_doc = jnp.concatenate([doc_col[other]] * (size // 128), axis=1)
            seen = key_doc == query_doc
            if other == block:
                key_at = lax.broadcasted_iota(jnp.int32, (size, size), 0)
                query_at = lax.broadcasted_iota(jnp.int32, (size, size), 1)
                seen = seen & (key_at <= query_at)
            scores = jnp.where(seen, scores, -1e30)
            score_buf[other] = scores
            top = jnp.max(scores, axis=0, keepdims=True)
            largest = top if largest is None else jnp.maximum(largest, top)
        total = jnp.zeros((1, size), jnp.float32)
        for other in range(block + 1):
            weights = jnp.exp2((score_buf[other] - largest) * (scaling * LOG2E))
            score_buf[other] = weights
            total = total + jnp.sum(weights, axis=0, keepdims=True)
        inverse = 1.0 / total
        wait_in(VALUE, block)
        value_t[block] = full[VALUE, rows_of(block)].astype(jnp.float32).T.astype(jnp.bfloat16)
        key_t[block] = full[KEY, rows_of(block)].astype(jnp.float32).T.astype(jnp.bfloat16)
        accum = jnp.zeros((head_size, size), jnp.float32)
        for other in range(block + 1):
            probs = (score_buf[other] * inverse).astype(jnp.bfloat16)
            prob_buf[block, other] = probs
            accum = accum + jnp.dot(value_t[other], probs, preferred_element_type=jnp.float32)
        rounded = accum.astype(jnp.bfloat16).astype(jnp.float32)
        out_t[block] = rounded
        ready[OUT, rows_of(block)] = rounded.T.astype(jnp.bfloat16)
        send_out(OUT, block)

    for block in reversed(range(blocks)):
        wait_in(GRAD, block)
        queries = full[QUERY, rows_of(block)]
        grads = full[GRAD, rows_of(block)]
        delta = jnp.sum(grads.astype(jnp.float32).T * out_t[block], axis=0, keepdims=True)
        accum = jnp.zeros((head_size, size), jnp.float32)
        for other in range(block + 1):
            probs = prob_buf[block, other]
            dprobs = nt_dot(full[VALUE, rows_of(other)], grads)
            dscores = (probs.astype(jnp.float32) * (dprobs - delta)).astype(jnp.bfloat16)
            value_part = jnp.dot(probs, grads, preferred_element_type=jnp.float32)
            key_part = jnp.dot(dscores, queries, preferred_element_type=jnp.float32)
            if block < blocks - 1:
                value_part = value_part + value_acc[other]
                key_part = key_part + key_acc[other]
            if other < block:
                value_acc[other] = value_part
                key_acc[other] = key_part
            else:
                ready[DV, rows_of(block)] = value_part.astype(jnp.bfloat16)
                ready[DK, rows_of(block)] = (scaling * key_part).astype(jnp.bfloat16)
            accum = accum + jnp.dot(key_t[other], dscores, preferred_element_type=jnp.float32)
        ready[DQ, rows_of(block)] = (scaling * accum).T.astype(jnp.bfloat16)
        for kind in (DV, DK, DQ):
            send_out(kind, block)

    for kind, part in ((VALUE, 1), (GRAD, 1), (GRAD, 0)):
        sent_in(kind, part)

    def drain_out(index, carry):
        owner = jnp.where(index < shards, index, 2 * shards - 1 - index)

        @pl.when(owner != me)
        def _():
            for kind in range(4):
                left = ready.at[kind, block_rows(index)]
                pltpu.make_async_copy(left, left, out_send.at[kind, index]).wait()

        return carry

    lax.fori_loop(0, 2 * shards, drain_out, 0)

    def collect(source, carry):
        for kind in range(4):
            for part in range(2):
                place = out_ref.at[kind, source, part_rows(part)]
                pltpu.make_async_copy(place, place, out_recv.at[kind, part, source]).wait()
        return carry

    lax.fori_loop(0, shards, collect, 0)


def rows_kernel(heads_ref, out_a, out_b, out_c, out_d, held, wide, turned, in_sem, out_sem):
    heads, rows, head_size = held.shape[1:]
    outs = (out_a, out_b, out_c, out_d)
    reads = [
        pltpu.make_async_copy(heads_ref.at[kind], held.at[kind], in_sem.at[kind])
        for kind in range(4)
    ]
    writes = [
        pltpu.make_async_copy(turned.at[kind], outs[kind], out_sem.at[kind]) for kind in range(4)
    ]
    for read in reads:
        read.start()
    for kind in range(4):
        reads[kind].wait()
        for head in range(heads):
            wide[pl.ds(head, rows, stride=heads), :] = held[kind, head].astype(jnp.float32)
        turned[kind] = wide[...].reshape(rows, heads, head_size).astype(jnp.bfloat16)
        writes[kind].start()
    for write in writes:
        write.wait()


def by_heads(queries, key_vecs, value_vecs, out_grad, doc_ids):
    shard_rows, head_count, head_size = queries.shape
    shards = lax.axis_size("ctx")
    half = shard_rows // 2
    tokens = shard_rows * shards
    group = 4
    size = group * half
    blocks = tokens // size
    bf16, f32 = jnp.bfloat16, jnp.float32
    vmem = pl.BlockSpec(memory_space=pltpu.VMEM)
    flops = 7 * tokens * tokens * head_size
    results = pl.pallas_call(
        functools.partial(head_kernel, shards, half, group),
        out_shape=jax.ShapeDtypeStruct((4, shards, shard_rows, head_size), bf16),
        in_specs=[pl.BlockSpec(memory_space=pltpu.HBM)] * 4 + [vmem],
        out_specs=pl.BlockSpec(memory_space=pl.ANY),
        scratch_shapes=[
            pltpu.VMEM((4, shard_rows, shards, head_size), bf16),
            pltpu.VMEM((4, shards, shard_rows, head_size), bf16),
            pltpu.VMEM((tokens, head_size), f32),
            pltpu.VMEM((4, tokens, head_size), bf16),
            pltpu.VMEM((4, tokens, head_size), bf16),
            pltpu.VMEM((blocks, size, 128), f32),
            pltpu.VMEM((blocks, head_size, size), bf16),
            pltpu.VMEM((blocks, head_size, size), bf16),
            pltpu.VMEM((blocks, head_size, size), f32),
            pltpu.VMEM((blocks, size, size), f32),
            pltpu.VMEM((blocks, blocks, size, size), bf16),
            pltpu.VMEM((blocks, size, head_size), f32),
            pltpu.VMEM((blocks, size, head_size), f32),
            pltpu.SemaphoreType.DMA((4, 2, shards)),
            pltpu.SemaphoreType.DMA((4, 2 * shards)),
            pltpu.SemaphoreType.DMA((4, 2 * shards)),
            pltpu.SemaphoreType.DMA((4, 2, shards)),
            pltpu.SemaphoreType.DMA((4,)),
        ],
        compiler_params=pltpu.CompilerParams(
            collective_id=0, has_side_effects=True, vmem_limit_bytes=40 * 1024 * 1024
        ),
        cost_estimate=pl.CostEstimate(
            flops=flops, bytes_accessed=8 * queries.size * 2, transcendentals=tokens * tokens // 2
        ),
    )(key_vecs, queries, value_vecs, out_grad, doc_ids)
    rows_first = jax.ShapeDtypeStruct((shard_rows, shards, head_size), bf16)
    return pl.pallas_call(
        rows_kernel,
        out_shape=[rows_first] * 4,
        in_specs=[pl.BlockSpec(memory_space=pl.ANY)],
        out_specs=[pl.BlockSpec(memory_space=pl.ANY)] * 4,
        scratch_shapes=[
            pltpu.VMEM((4, shards, shard_rows, head_size), bf16),
            pltpu.VMEM((shard_rows * shards, head_size), f32),
            pltpu.VMEM((4, shard_rows, shards, head_size), bf16),
            pltpu.SemaphoreType.DMA((4,)),
            pltpu.SemaphoreType.DMA((4,)),
        ],
        compiler_params=pltpu.CompilerParams(vmem_limit_bytes=16 * 1024 * 1024),
        cost_estimate=pl.CostEstimate(
            flops=0, bytes_accessed=16 * queries.size, transcendentals=0
        ),
    )(results)


def on_device(queries, key_vecs, value_vecs, out_grad, doc_ids):
    shard_rows, head_count, head_size = queries.shape
    fits = (
        head_count == lax.axis_size("ctx")
        and shard_rows % 32 == 0
        and (2 * shard_rows) % 128 == 0
        and head_size == 128
    )
    attend = by_heads if fits else gathered
    return attend(queries, key_vecs, value_vecs, out_grad, doc_ids)


def solution(mesh):
    return jax.shard_map(
        on_device,
        mesh=mesh,
        in_specs=(
            P(("grp", "ctx"), "head", None),
            P(("grp", "ctx"), "head", None),
            P(("grp", "ctx"), "head", None),
            P(("grp", "ctx"), "head", None),
            P("grp"),
        ),
        out_specs=(
            P(("grp", "ctx"), "head", None),
            P(("grp", "ctx"), "head", None),
            P(("grp", "ctx"), "head", None),
            P(("grp", "ctx"), "head", None),
        ),
        check_vma=False,
    )
```

```python
import functools

import jax
import jax.numpy as jnp
from jax import lax
from jax.experimental import pallas as pl
from jax.experimental.pallas import tpu as pltpu
from jax.sharding import PartitionSpec as P


def block_length(shard_rows, shard_count):
    factor = 1
    while factor * shard_rows < 512 and shard_count % (factor * 2) == 0:
        factor = factor * 2
    return factor * shard_rows


def stored_position(rows, shard_rows, shard_count):
    half_rows = shard_rows // 2
    shard = rows // shard_rows
    within = rows % shard_rows
    return jnp.where(
        within < half_rows,
        shard * half_rows + within,
        (2 * shard_count - 1 - shard) * half_rows + within - half_rows,
    )


def score_block(query_blk, query_pos, query_doc, key_blk, key_pos, key_doc, scaling):
    scores = (
        jnp.einsum("qhd,khd->hqk", query_blk, key_blk, preferred_element_type=jnp.float32) * scaling
    )
    allowed = (key_doc[None, :] == query_doc[:, None]) & (key_pos[None, :] <= query_pos[:, None])
    return (scores, allowed[None])


def probs_of(scores, allowed, lse):
    return jnp.where(allowed, jnp.exp(scores - lse[:, :, None]), 0.0).astype(jnp.bfloat16)


def dscores_of(probs, grad_blk, value_blk, delta):
    dprobs = jnp.einsum("qhd,khd->hqk", grad_blk, value_blk, preferred_element_type=jnp.float32)
    return (probs.astype(jnp.float32) * (dprobs - delta[:, :, None])).astype(jnp.bfloat16)


def gathered(queries, key_vecs, value_vecs, out_grad, doc_ids):
    shard_rows = queries.shape[0]
    head_count = queries.shape[1]
    head_size = queries.shape[2]
    scaling = head_size ** (-0.5)
    shard_count = lax.axis_size("ctx")
    shard_index = lax.axis_index("ctx")
    own_start = shard_index * shard_rows

    def positions(start, length):
        return stored_position(start + jnp.arange(length, dtype=jnp.int32), shard_rows, shard_count)

    own_pos = positions(own_start, shard_rows)
    own_doc = jnp.take(doc_ids, own_pos)
    keys_all, values_all = (
        lax.all_gather(key_vecs, "ctx", axis=0, tiled=True),
        lax.all_gather(value_vecs, "ctx", axis=0, tiled=True),
    )
    block = block_length(shard_rows, shard_count)
    block_count = keys_all.shape[0] // block

    def key_slices(start, length):
        key_blk = lax.dynamic_slice_in_dim(keys_all, start, length, 0)
        value_blk = lax.dynamic_slice_in_dim(values_all, start, length, 0)
        key_pos = positions(start, length)
        key_doc = jnp.take(doc_ids, key_pos)
        return (key_blk, value_blk, key_pos, key_doc)

    def stat_step(index, carry):
        running, total = carry
        key_blk, value_blk, key_pos, key_doc = key_slices(index * block, block)
        scores, allowed = score_block(queries, own_pos, own_doc, key_blk, key_pos, key_doc, scaling)
        newmax = jnp.maximum(running, jnp.max(jnp.where(allowed, scores, -1e30), axis=-1))
        total = total * jnp.exp(running - newmax) + jnp.sum(
            jnp.where(allowed, jnp.exp(scores - newmax[:, :, None]), 0.0), axis=-1
        )
        return (newmax, total)

    start_max = jnp.full((head_count, shard_rows), -1e30, jnp.float32)
    start_sum = jnp.zeros((head_count, shard_rows), jnp.float32)
    running, total = lax.fori_loop(0, block_count, stat_step, (start_max, start_sum))
    lse = running + jnp.log(total)

    def out_step(index, accum):
        key_blk, value_blk, key_pos, key_doc = key_slices(index * block, block)
        scores, allowed = score_block(queries, own_pos, own_doc, key_blk, key_pos, key_doc, scaling)
        probs = probs_of(scores, allowed, lse)
        return accum + jnp.einsum(
            "hqk,khd->qhd", probs, value_blk, preferred_element_type=jnp.float32
        )

    zero_rows = jnp.zeros((shard_rows, head_count, head_size), jnp.float32)
    attn_out = lax.fori_loop(0, block_count, out_step, zero_rows).astype(jnp.bfloat16)
    delta_rows = jnp.sum(out_grad.astype(jnp.float32) * attn_out.astype(jnp.float32), axis=-1)
    delta = delta_rows.T

    def query_step(index, accum):
        key_blk, value_blk, key_pos, key_doc = key_slices(index * block, block)
        scores, allowed = score_block(queries, own_pos, own_doc, key_blk, key_pos, key_doc, scaling)
        probs = probs_of(scores, allowed, lse)
        dscores = dscores_of(probs, out_grad, value_blk, delta)
        return accum + jnp.einsum(
            "hqk,khd->qhd", dscores, key_blk, preferred_element_type=jnp.float32
        )

    query_grad = (scaling * lax.fori_loop(0, block_count, query_step, zero_rows)).astype(
        jnp.bfloat16
    )
    lse_all, delta_all = (
        lax.all_gather(lse.T, "ctx", axis=0, tiled=True),
        lax.all_gather(delta_rows, "ctx", axis=0, tiled=True),
    )
    query_blk = lax.all_gather(queries, "ctx", axis=0, tiled=True)
    grad_blk = lax.all_gather(out_grad, "ctx", axis=0, tiled=True)
    length = query_blk.shape[0]
    query_pos = positions(jnp.int32(0), length)
    query_doc = jnp.take(doc_ids, query_pos)
    lse_blk = lse_all.T
    delta_blk = delta_all.T
    scores, allowed = score_block(
        query_blk, query_pos, query_doc, key_vecs, own_pos, own_doc, scaling
    )
    probs = probs_of(scores, allowed, lse_blk)
    dscores = dscores_of(probs, grad_blk, value_vecs, delta_blk)
    key_accum = scaling * jnp.einsum(
        "hqk,qhd->khd", dscores, query_blk, preferred_element_type=jnp.float32
    )
    value_accum = jnp.einsum("hqk,qhd->khd", probs, grad_blk, preferred_element_type=jnp.float32)
    key_grad = key_accum.astype(jnp.bfloat16)
    value_grad = value_accum.astype(jnp.bfloat16)
    return (attn_out, query_grad, key_grad, value_grad)


KEY, QUERY, VALUE, GRAD = 0, 1, 2, 3
OUT, DQ, DK, DV = 0, 1, 2, 3
VMEM_BYTES = 62 * 1024 * 1024 + 600 * 1024
LOG2E = 1.4426950408889634


def nt_dot(a, b):
    return lax.dot_general(a, b, (((1,), (1,)), ((), ())), preferred_element_type=jnp.float32)


def head_kernel(
    shards,
    half,
    group,
    key_ref,
    query_ref,
    value_ref,
    grad_ref,
    doc_ref,
    out_ref,
    more_ref,
    fetched,
    staged,
    wide,
    full,
    ready,
    zeros,
    doc_col,
    key_t,
    value_t,
    out_t,
    score_buf,
    prob_buf,
    key_acc,
    value_acc,
    in_send,
    in_recv,
    out_send,
    out_recv,
    fetch_sem,
    low_send,
    more_send,
    more_recv,
    zero_sem,
):
    me = lax.axis_index("ctx")
    lower = shards // 2
    low = me < lower
    size = half * group
    blocks = 2 * shards // group
    head_size = full.shape[-1]
    scaling = head_size ** (-0.5)

    fetches = [
        pltpu.make_async_copy(ref, fetched.at[kind], fetch_sem.at[kind])
        for kind, ref in ((KEY, key_ref), (QUERY, query_ref), (VALUE, value_ref), (GRAD, grad_ref))
    ]
    for fetch in fetches:
        fetch.start()

    barrier = pltpu.get_barrier_semaphore()

    def greet(step, carry):
        pl.semaphore_signal(
            barrier,
            inc=1,
            device_id={"ctx": lax.rem(me + step, shards)},
            device_id_type=pl.DeviceIdType.MESH,
        )
        return carry

    lax.fori_loop(1, shards, greet, 0)

    def stage(kind):
        fetches[kind].wait()
        rows = fetched.shape[1]
        wide[...] = fetched[kind].astype(jnp.float32).reshape(rows * shards, head_size)
        for head in range(shards):
            staged[kind, head] = wide[pl.ds(head, rows, stride=shards), :].astype(jnp.bfloat16)

    def part_rows(part):
        return pl.ds(part * half, half)

    def block_rows(index):
        return pl.ds(pl.multiple_of(index * half, half), half)

    def position(part):
        return me if part == 0 else 2 * shards - 1 - me

    def far_first(step):
        return lax.rem(step + shards // 2 - 2, shards - 1) + 1

    def stays_low(kind, part, target):
        if part == 1 or kind in (KEY, VALUE):
            return None
        return low & (target >= lower)

    def unless(skip, act):
        if skip is None:
            act()
        else:
            pl.when(jnp.logical_not(skip))(act)

    def sent_in(kind, part):
        def one(step, carry):
            target = lax.rem(me + far_first(step), shards)

            def act():
                left = staged.at[kind, target, part_rows(part)]
                pltpu.make_async_copy(left, left, in_send.at[kind, part, step]).wait()

            unless(stays_low(kind, part, target), act)
            return carry

        lax.fori_loop(1, shards, one, 0)

    def send_in(kind, part):
        where = position(part)
        pltpu.make_async_copy(
            staged.at[kind, me, part_rows(part)],
            full.at[kind, block_rows(where)],
            in_recv.at[kind, where],
        ).start()

        def one(step, carry):
            target = lax.rem(me + far_first(step), shards)

            def act():
                pltpu.make_async_remote_copy(
                    src_ref=staged.at[kind, target, part_rows(part)],
                    dst_ref=full.at[kind, block_rows(where)],
                    send_sem=in_send.at[kind, part, step],
                    recv_sem=in_recv.at[kind, where],
                    device_id={"ctx": target},
                    device_id_type=pl.DeviceIdType.MESH,
                ).start()

            unless(stays_low(kind, part, target), act)
            return carry

        lax.fori_loop(1, shards, one, 0)

    def send_low(kind):
        where = 2 * shards + me

        @pl.when(low)
        def _():
            pltpu.make_async_copy(
                staged.at[kind, me + lower, part_rows(0)],
                full.at[kind, block_rows(where)],
                in_recv.at[kind, where],
            ).start()

            def one(step, carry):
                target = lax.rem(me + step, lower)
                pltpu.make_async_remote_copy(
                    src_ref=staged.at[kind, target + lower, part_rows(0)],
                    dst_ref=full.at[kind, block_rows(where)],
                    send_sem=low_send.at[kind, step],
                    recv_sem=in_recv.at[kind, where],
                    device_id={"ctx": target},
                    device_id_type=pl.DeviceIdType.MESH,
                ).start()
                return carry

            lax.fori_loop(1, lower, one, 0)

    def wait_in(kind, block):
        def one(index, carry):
            held = full.at[kind, block_rows(index)]
            pltpu.make_async_copy(held, held, in_recv.at[kind, index]).wait()
            return carry

        lax.fori_loop(block * group, (block + 1) * group, one, 0)

    def send_piece(held, place, owner, send_sem, recv_sem):
        @pl.when(owner == me)
        def _():
            pltpu.make_async_copy(held, place, recv_sem).start()

        @pl.when(owner != me)
        def _():
            pltpu.make_async_remote_copy(
                src_ref=held,
                dst_ref=place,
                send_sem=send_sem,
                recv_sem=recv_sem,
                device_id={"ctx": owner},
                device_id_type=pl.DeviceIdType.MESH,
            ).start()

    def send_out(kind, block):
        for index in range(block * group, (block + 1) * group):
            part = 0 if index < shards else 1
            owner = index if part == 0 else 2 * shards - 1 - index
            send_piece(
                ready.at[kind, pl.ds(index * half, half)],
                out_ref.at[kind, me, part_rows(part)],
                owner,
                out_send.at[kind, index],
                out_recv.at[kind, part, me],
            )

    def send_more(kind):
        for index in range(lower):
            held = ready.at[kind, pl.ds((2 * shards + index) * half, half)]
            if kind in (OUT, DQ):
                place = out_ref.at[kind, me + lower, part_rows(0)]
                recv_sem = out_recv.at[kind, 0, me + lower]
            else:
                place = more_ref.at[kind - DK, me]
                recv_sem = more_recv.at[kind - DK, me]
            send_piece(held, place, index, more_send.at[kind, index], recv_sem)

    stage(KEY)
    pl.semaphore_wait(barrier, shards - 1)
    send_in(KEY, 0)
    stage(QUERY)
    send_in(QUERY, 0)
    stage(VALUE)
    send_in(VALUE, 0)
    for kind in (KEY, QUERY, VALUE):
        send_low(kind)
    stage(GRAD)

    docs = doc_ref[...].astype(jnp.float32).reshape(1, -1)
    for block in range(blocks):
        piece = docs[:, block * size : (block + 1) * size]
        doc_col[block] = jnp.broadcast_to(piece, (128, size)).T

    for kind in (KEY, QUERY, VALUE):
        sent_in(kind, 0)
        send_in(kind, 1)

    def rows_of(block):
        return pl.ds(block * size, size)

    def turn_keys(block):
        value_t[block] = full[VALUE, rows_of(block)].astype(jnp.float32).T.astype(jnp.bfloat16)
        key_t[block] = full[KEY, rows_of(block)].astype(jnp.float32).T.astype(jnp.bfloat16)

    def send_block(kind, block):
        if block == blocks:
            send_more(kind)
        else:
            send_out(kind, block)

    def keys_of(block):
        return [block] if block == blocks else list(reversed(range(block + 1)))

    def forward(block):
        keys = keys_of(block)
        wait_in(KEY, block)
        wait_in(QUERY, block)
        queries = full[QUERY, rows_of(block)]
        at = block % blocks * size
        query_doc = docs[:, at : at + size]
        largest = None
        for other in keys:
            scores = nt_dot(full[KEY, rows_of(other)], queries)
            key_doc = jnp.concatenate([doc_col[other % blocks]] * (size // 128), axis=1)
            seen = key_doc == query_doc
            if other == block:
                key_at = lax.broadcasted_iota(jnp.int32, (size, size), 0)
                query_at = lax.broadcasted_iota(jnp.int32, (size, size), 1)
                seen = seen & (key_at <= query_at)
            scores = jnp.where(seen, scores, -1e30)
            score_buf[other % blocks] = scores
            top = jnp.max(scores, axis=0, keepdims=True)
            largest = top if largest is None else jnp.maximum(largest, top)
        total = jnp.zeros((1, size), jnp.float32)
        for other in keys:
            weights = jnp.exp2((score_buf[other % blocks] - largest) * (scaling * LOG2E))
            score_buf[other % blocks] = weights
            total = total + jnp.sum(weights, axis=0, keepdims=True)
        inverse = 1.0 / total
        wait_in(VALUE, block)
        turn_keys(block)
        accum = jnp.zeros((head_size, size), jnp.float32)
        for other in keys:
            probs = (score_buf[other % blocks] * inverse).astype(jnp.bfloat16)
            prob_buf[block, other % blocks] = probs
            accum = accum + jnp.dot(value_t[other], probs, preferred_element_type=jnp.float32)
        rounded = accum.astype(jnp.bfloat16).astype(jnp.float32)
        out_t[block] = rounded
        ready[OUT, rows_of(block)] = rounded.T.astype(jnp.bfloat16)
        send_block(OUT, block)

    def backward(block):
        keys = keys_of(block)
        wait_in(GRAD, block)
        queries = full[QUERY, rows_of(block)]
        grads = full[GRAD, rows_of(block)]
        delta = jnp.sum(grads.astype(jnp.float32).T * out_t[block], axis=0, keepdims=True)
        accum = jnp.zeros((head_size, size), jnp.float32)
        for other in keys:
            probs = prob_buf[block, other % blocks]
            dprobs = nt_dot(full[VALUE, rows_of(other)], grads)
            dscores = (probs.astype(jnp.float32) * (dprobs - delta)).astype(jnp.bfloat16)
            value_part = jnp.dot(probs, grads, preferred_element_type=jnp.float32)
            key_part = jnp.dot(dscores, queries, preferred_element_type=jnp.float32)
            if block < blocks - 1:
                value_part = value_part + value_acc[other]
                key_part = key_part + key_acc[other]
            if other < block:
                value_acc[other] = value_part
                key_acc[other] = key_part
            else:
                finish_keys(block, value_part, key_part)
            accum = accum + jnp.dot(key_t[other], dscores, preferred_element_type=jnp.float32)
        ready[DQ, rows_of(block)] = (scaling * accum).T.astype(jnp.bfloat16)
        send_block(DQ, block)

    def finish_keys(block, value_part, key_part):
        ready[DV, rows_of(block)] = value_part.astype(jnp.bfloat16)
        send_block(DV, block)
        ready[DK, rows_of(block)] = (scaling * key_part).astype(jnp.bfloat16)
        send_block(DK, block)

    @pl.when(low)
    def _():
        forward(0)

    @pl.when(jnp.logical_not(low))
    def _():
        zeros[...] = jnp.zeros_like(zeros)
        pltpu.make_async_copy(zeros, more_ref, zero_sem).start()
        wait_in(KEY, 0)
        wait_in(VALUE, 0)
        turn_keys(0)

    for block in range(1, blocks):
        if block == blocks // 2:
            for kind, part in ((KEY, 1), (QUERY, 0)):
                sent_in(kind, 1)
                send_in(GRAD, part)
            send_low(GRAD)

            @pl.when(low)
            def _():
                forward(blocks)

        forward(block)

    for block in reversed(range(1, blocks)):
        backward(block)

    @pl.when(low)
    def _():
        backward(0)
        backward(blocks)

    @pl.when(jnp.logical_not(low))
    def _():
        finish_keys(0, value_acc[0], key_acc[0])
        pltpu.make_async_copy(zeros, more_ref, zero_sem).wait()

    for kind, part in ((VALUE, 1), (GRAD, 1), (GRAD, 0)):
        sent_in(kind, part)

    @pl.when(low)
    def _():
        def drain_low(step, carry):
            for kind in range(4):
                left = staged.at[kind, lax.rem(me + step, lower) + lower, part_rows(0)]
                pltpu.make_async_copy(left, left, low_send.at[kind, step]).wait()
            return carry

        lax.fori_loop(1, lower, drain_low, 0)

        def drain_more(index, carry):
            @pl.when(index != me)
            def _():
                for kind in range(4):
                    left = ready.at[kind, block_rows(2 * shards + index)]
                    pltpu.make_async_copy(left, left, more_send.at[kind, index]).wait()

            return carry

        lax.fori_loop(0, lower, drain_more, 0)

        def collect_more(source, carry):
            for kind in range(2):
                place = more_ref.at[kind, source]
                pltpu.make_async_copy(place, place, more_recv.at[kind, source]).wait()
            return carry

        lax.fori_loop(0, lower, collect_more, 0)

    def drain_out(index, carry):
        owner = jnp.where(index < shards, index, 2 * shards - 1 - index)

        @pl.when(owner != me)
        def _():
            for kind in range(4):

                def act():
                    left = ready.at[kind, block_rows(index)]
                    pltpu.make_async_copy(left, left, out_send.at[kind, index]).wait()

                kept = jnp.logical_not(low) & (index < lower) if kind in (OUT, DQ) else None
                unless(kept, act)

        return carry

    lax.fori_loop(0, 2 * shards, drain_out, 0)

    def collect(source, carry):
        for kind in range(4):
            for part in range(2):
                place = out_ref.at[kind, source, part_rows(part)]
                pltpu.make_async_copy(place, place, out_recv.at[kind, part, source]).wait()
        return carry

    lax.fori_loop(0, shards, collect, 0)


def rows_kernel(
    heads_ref, more_ref, out_a, out_b, out_c, out_d, held, more, wide, turned, in_sem, out_sem
):
    heads, rows, head_size = held.shape[1:]
    outs = (out_a, out_b, out_c, out_d)
    reads = [
        pltpu.make_async_copy(heads_ref.at[kind], held.at[kind], in_sem.at[kind])
        for kind in range(4)
    ]
    writes = [
        pltpu.make_async_copy(turned.at[kind], outs[kind], out_sem.at[kind]) for kind in range(4)
    ]
    lower, half = more.shape[1:3]
    late = pltpu.make_async_copy(more_ref, more, in_sem.at[4])
    late.start()
    for read in reads:
        read.start()
    for kind in range(4):
        reads[kind].wait()
        if kind == DK:
            late.wait()
        for head in range(heads):
            wide[pl.ds(head, rows, stride=heads), :] = held[kind, head].astype(jnp.float32)
        if kind in (DK, DV):
            for head in range(lower, heads):
                first = pl.ds(head, half, stride=heads)
                wide[first, :] = wide[first, :] + more[kind - DK, head - lower].astype(jnp.float32)
        turned[kind] = wide[...].reshape(rows, heads, head_size).astype(jnp.bfloat16)
        writes[kind].start()
    for write in writes:
        write.wait()


def by_heads(queries, key_vecs, value_vecs, out_grad, doc_ids):
    shard_rows, head_count, head_size = queries.shape
    shards = lax.axis_size("ctx")
    half = shard_rows // 2
    tokens = shard_rows * shards
    group = 4
    size = group * half
    blocks = tokens // size
    bf16, f32 = jnp.bfloat16, jnp.float32
    vmem = pl.BlockSpec(memory_space=pltpu.VMEM)
    flops = 7 * tokens * tokens * head_size
    results, more = pl.pallas_call(
        functools.partial(head_kernel, shards, half, group),
        out_shape=[
            jax.ShapeDtypeStruct((4, shards, shard_rows, head_size), bf16),
            jax.ShapeDtypeStruct((2, shards // 2, half, head_size), bf16),
        ],
        in_specs=[pl.BlockSpec(memory_space=pltpu.HBM)] * 4 + [vmem],
        out_specs=[pl.BlockSpec(memory_space=pl.ANY)] * 2,
        scratch_shapes=[
            pltpu.VMEM((4, shard_rows, shards, head_size), bf16),
            pltpu.VMEM((4, shards, shard_rows, head_size), bf16),
            pltpu.VMEM((tokens, head_size), f32),
            pltpu.VMEM((4, tokens + size, head_size), bf16),
            pltpu.VMEM((4, tokens + size, head_size), bf16),
            pltpu.VMEM((2, shards // 2, half, head_size), bf16),
            pltpu.VMEM((blocks, size, 128), f32),
            pltpu.VMEM((blocks + 1, head_size, size), bf16),
            pltpu.VMEM((blocks + 1, head_size, size), bf16),
            pltpu.VMEM((blocks + 1, head_size, size), f32),
            pltpu.VMEM((blocks, size, size), f32),
            pltpu.VMEM((blocks + 1, blocks, size, size), bf16),
            pltpu.VMEM((blocks, size, head_size), f32),
            pltpu.VMEM((blocks, size, head_size), f32),
            pltpu.SemaphoreType.DMA((4, 2, shards)),
            pltpu.SemaphoreType.DMA((4, 2 * shards + shards // 2)),
            pltpu.SemaphoreType.DMA((4, 2 * shards)),
            pltpu.SemaphoreType.DMA((4, 2, shards)),
            pltpu.SemaphoreType.DMA((4,)),
            pltpu.SemaphoreType.DMA((4, shards // 2)),
            pltpu.SemaphoreType.DMA((4, shards // 2)),
            pltpu.SemaphoreType.DMA((2, shards // 2)),
            pltpu.SemaphoreType.DMA,
        ],
        compiler_params=pltpu.CompilerParams(
            collective_id=0, has_side_effects=True, vmem_limit_bytes=VMEM_BYTES
        ),
        cost_estimate=pl.CostEstimate(
            flops=flops, bytes_accessed=8 * queries.size * 2, transcendentals=tokens * tokens // 2
        ),
    )(key_vecs, queries, value_vecs, out_grad, doc_ids)
    rows_first = jax.ShapeDtypeStruct((shard_rows, shards, head_size), bf16)
    return pl.pallas_call(
        rows_kernel,
        out_shape=[rows_first] * 4,
        in_specs=[pl.BlockSpec(memory_space=pl.ANY)] * 2,
        out_specs=[pl.BlockSpec(memory_space=pl.ANY)] * 4,
        scratch_shapes=[
            pltpu.VMEM((4, shards, shard_rows, head_size), bf16),
            pltpu.VMEM((2, shards // 2, half, head_size), bf16),
            pltpu.VMEM((shard_rows * shards, head_size), f32),
            pltpu.VMEM((4, shard_rows, shards, head_size), bf16),
            pltpu.SemaphoreType.DMA((5,)),
            pltpu.SemaphoreType.DMA((4,)),
        ],
        compiler_params=pltpu.CompilerParams(vmem_limit_bytes=16 * 1024 * 1024),
        cost_estimate=pl.CostEstimate(
            flops=0, bytes_accessed=16 * queries.size, transcendentals=0
        ),
    )(results, more)


def on_device(queries, key_vecs, value_vecs, out_grad, doc_ids):
    shard_rows, head_count, head_size = queries.shape
    fits = (
        head_count == lax.axis_size("ctx")
        and head_count == 8
        and shard_rows % 32 == 0
        and (2 * shard_rows) % 128 == 0
        and head_size == 128
    )
    attend = by_heads if fits else gathered
    return attend(queries, key_vecs, value_vecs, out_grad, doc_ids)


def solution(mesh):
    return jax.shard_map(
        on_device,
        mesh=mesh,
        in_specs=(
            P(("grp", "ctx"), "head", None),
            P(("grp", "ctx"), "head", None),
            P(("grp", "ctx"), "head", None),
            P(("grp", "ctx"), "head", None),
            P("grp"),
        ),
        out_specs=(
            P(("grp", "ctx"), "head", None),
            P(("grp", "ctx"), "head", None),
            P(("grp", "ctx"), "head", None),
            P(("grp", "ctx"), "head", None),
        ),
        check_vma=False,
    )
```

```python
import functools

import jax
import jax.numpy as jnp
from jax import lax
from jax.experimental import pallas as pl
from jax.experimental.pallas import tpu as pltpu
from jax.sharding import PartitionSpec as P


def block_length(shard_rows, shard_count):
    factor = 1
    while factor * shard_rows < 512 and shard_count % (factor * 2) == 0:
        factor = factor * 2
    return factor * shard_rows


def stored_position(rows, shard_rows, shard_count):
    half_rows = shard_rows // 2
    shard = rows // shard_rows
    within = rows % shard_rows
    return jnp.where(
        within < half_rows,
        shard * half_rows + within,
        (2 * shard_count - 1 - shard) * half_rows + within - half_rows,
    )


def score_block(query_blk, query_pos, query_doc, key_blk, key_pos, key_doc, scaling):
    scores = (
        jnp.einsum("qhd,khd->hqk", query_blk, key_blk, preferred_element_type=jnp.float32) * scaling
    )
    allowed = (key_doc[None, :] == query_doc[:, None]) & (key_pos[None, :] <= query_pos[:, None])
    return (scores, allowed[None])


def probs_of(scores, allowed, lse):
    return jnp.where(allowed, jnp.exp(scores - lse[:, :, None]), 0.0).astype(jnp.bfloat16)


def dscores_of(probs, grad_blk, value_blk, delta):
    dprobs = jnp.einsum("qhd,khd->hqk", grad_blk, value_blk, preferred_element_type=jnp.float32)
    return (probs.astype(jnp.float32) * (dprobs - delta[:, :, None])).astype(jnp.bfloat16)


def gathered(queries, key_vecs, value_vecs, out_grad, doc_ids):
    shard_rows = queries.shape[0]
    head_count = queries.shape[1]
    head_size = queries.shape[2]
    scaling = head_size ** (-0.5)
    shard_count = lax.axis_size("ctx")
    shard_index = lax.axis_index("ctx")
    own_start = shard_index * shard_rows

    def positions(start, length):
        return stored_position(start + jnp.arange(length, dtype=jnp.int32), shard_rows, shard_count)

    own_pos = positions(own_start, shard_rows)
    own_doc = jnp.take(doc_ids, own_pos)
    keys_all, values_all = (
        lax.all_gather(key_vecs, "ctx", axis=0, tiled=True),
        lax.all_gather(value_vecs, "ctx", axis=0, tiled=True),
    )
    block = block_length(shard_rows, shard_count)
    block_count = keys_all.shape[0] // block

    def key_slices(start, length):
        key_blk = lax.dynamic_slice_in_dim(keys_all, start, length, 0)
        value_blk = lax.dynamic_slice_in_dim(values_all, start, length, 0)
        key_pos = positions(start, length)
        key_doc = jnp.take(doc_ids, key_pos)
        return (key_blk, value_blk, key_pos, key_doc)

    def stat_step(index, carry):
        running, total = carry
        key_blk, value_blk, key_pos, key_doc = key_slices(index * block, block)
        scores, allowed = score_block(queries, own_pos, own_doc, key_blk, key_pos, key_doc, scaling)
        newmax = jnp.maximum(running, jnp.max(jnp.where(allowed, scores, -1e30), axis=-1))
        total = total * jnp.exp(running - newmax) + jnp.sum(
            jnp.where(allowed, jnp.exp(scores - newmax[:, :, None]), 0.0), axis=-1
        )
        return (newmax, total)

    start_max = jnp.full((head_count, shard_rows), -1e30, jnp.float32)
    start_sum = jnp.zeros((head_count, shard_rows), jnp.float32)
    running, total = lax.fori_loop(0, block_count, stat_step, (start_max, start_sum))
    lse = running + jnp.log(total)

    def out_step(index, accum):
        key_blk, value_blk, key_pos, key_doc = key_slices(index * block, block)
        scores, allowed = score_block(queries, own_pos, own_doc, key_blk, key_pos, key_doc, scaling)
        probs = probs_of(scores, allowed, lse)
        return accum + jnp.einsum(
            "hqk,khd->qhd", probs, value_blk, preferred_element_type=jnp.float32
        )

    zero_rows = jnp.zeros((shard_rows, head_count, head_size), jnp.float32)
    attn_out = lax.fori_loop(0, block_count, out_step, zero_rows).astype(jnp.bfloat16)
    delta_rows = jnp.sum(out_grad.astype(jnp.float32) * attn_out.astype(jnp.float32), axis=-1)
    delta = delta_rows.T

    def query_step(index, accum):
        key_blk, value_blk, key_pos, key_doc = key_slices(index * block, block)
        scores, allowed = score_block(queries, own_pos, own_doc, key_blk, key_pos, key_doc, scaling)
        probs = probs_of(scores, allowed, lse)
        dscores = dscores_of(probs, out_grad, value_blk, delta)
        return accum + jnp.einsum(
            "hqk,khd->qhd", dscores, key_blk, preferred_element_type=jnp.float32
        )

    query_grad = (scaling * lax.fori_loop(0, block_count, query_step, zero_rows)).astype(
        jnp.bfloat16
    )
    lse_all, delta_all = (
        lax.all_gather(lse.T, "ctx", axis=0, tiled=True),
        lax.all_gather(delta_rows, "ctx", axis=0, tiled=True),
    )
    query_blk = lax.all_gather(queries, "ctx", axis=0, tiled=True)
    grad_blk = lax.all_gather(out_grad, "ctx", axis=0, tiled=True)
    length = query_blk.shape[0]
    query_pos = positions(jnp.int32(0), length)
    query_doc = jnp.take(doc_ids, query_pos)
    lse_blk = lse_all.T
    delta_blk = delta_all.T
    scores, allowed = score_block(
        query_blk, query_pos, query_doc, key_vecs, own_pos, own_doc, scaling
    )
    probs = probs_of(scores, allowed, lse_blk)
    dscores = dscores_of(probs, grad_blk, value_vecs, delta_blk)
    key_accum = scaling * jnp.einsum(
        "hqk,qhd->khd", dscores, query_blk, preferred_element_type=jnp.float32
    )
    value_accum = jnp.einsum("hqk,qhd->khd", probs, grad_blk, preferred_element_type=jnp.float32)
    key_grad = key_accum.astype(jnp.bfloat16)
    value_grad = value_accum.astype(jnp.bfloat16)
    return (attn_out, query_grad, key_grad, value_grad)


KEY, QUERY, VALUE, GRAD = 0, 1, 2, 3
OUT, DQ, DK, DV = 0, 1, 2, 3
VMEM_BYTES = 62 * 1024 * 1024 + 600 * 1024
LOG2E = 1.4426950408889634


def nt_dot(a, b):
    return lax.dot_general(a, b, (((1,), (1,)), ((), ())), preferred_element_type=jnp.float32)


def head_kernel(
    shards,
    half,
    group,
    key_ref,
    query_ref,
    value_ref,
    grad_ref,
    doc_ref,
    out_ref,
    more_ref,
    fetched,
    staged,
    wide,
    full,
    ready,
    zeros,
    doc_col,
    key_t,
    value_t,
    out_t,
    score_buf,
    prob_buf,
    key_acc,
    value_acc,
    in_send,
    in_recv,
    out_send,
    out_recv,
    fetch_sem,
    low_send,
    more_send,
    more_recv,
    help_send,
    zero_sem,
):
    me = lax.axis_index("ctx")
    lower = shards // 2
    low = me < lower
    helpers = lower // 2
    helped = me < helpers
    helping = (me >= lower) & (me < lower + helpers)
    size = half * group
    blocks = 2 * shards // group
    head_size = full.shape[-1]
    scaling = head_size ** (-0.5)

    fetches = [
        pltpu.make_async_copy(ref, fetched.at[kind], fetch_sem.at[kind])
        for kind, ref in ((KEY, key_ref), (QUERY, query_ref), (VALUE, value_ref), (GRAD, grad_ref))
    ]
    for fetch in fetches:
        fetch.start()

    barrier = pltpu.get_barrier_semaphore()

    def greet(step, carry):
        pl.semaphore_signal(
            barrier,
            inc=1,
            device_id={"ctx": lax.rem(me + step, shards)},
            device_id_type=pl.DeviceIdType.MESH,
        )
        return carry

    lax.fori_loop(1, shards, greet, 0)

    def stage(kind):
        fetches[kind].wait()
        rows = fetched.shape[1]
        wide[...] = fetched[kind].astype(jnp.float32).reshape(rows * shards, head_size)
        for head in range(shards):
            staged[kind, head] = wide[pl.ds(head, rows, stride=shards), :].astype(jnp.bfloat16)

    def part_rows(part):
        return pl.ds(part * half, half)

    def block_rows(index):
        return pl.ds(pl.multiple_of(index * half, half), half)

    def position(part):
        return me if part == 0 else 2 * shards - 1 - me

    def far_first(step):
        return lax.rem(step + shards // 2 - 2, shards - 1) + 1

    def diverted(kind, part, target):
        if part == 1 or kind in (KEY, VALUE):
            return None
        return (low & (target >= lower)) | ((me >= lower) & (target < helpers))

    def unless(skip, act):
        if skip is None:
            act()
        else:
            pl.when(jnp.logical_not(skip))(act)

    def sent_in(kind, part):
        def one(step, carry):
            target = lax.rem(me + far_first(step), shards)

            def act():
                left = staged.at[kind, target, part_rows(part)]
                pltpu.make_async_copy(left, left, in_send.at[kind, part, step]).wait()

            unless(diverted(kind, part, target), act)
            return carry

        lax.fori_loop(1, shards, one, 0)

    def send_in(kind, part):
        where = position(part)
        pltpu.make_async_copy(
            staged.at[kind, me, part_rows(part)],
            full.at[kind, block_rows(where)],
            in_recv.at[kind, where],
        ).start()

        def one(step, carry):
            target = lax.rem(me + far_first(step), shards)

            def act():
                pltpu.make_async_remote_copy(
                    src_ref=staged.at[kind, target, part_rows(part)],
                    dst_ref=full.at[kind, block_rows(where)],
                    send_sem=in_send.at[kind, part, step],
                    recv_sem=in_recv.at[kind, where],
                    device_id={"ctx": target},
                    device_id_type=pl.DeviceIdType.MESH,
                ).start()

            unless(diverted(kind, part, target), act)
            return carry

        lax.fori_loop(1, shards, one, 0)

    def send_low(kind):
        where = 2 * shards + me

        @pl.when(low)
        def _():
            pltpu.make_async_copy(
                staged.at[kind, me + lower, part_rows(0)],
                full.at[kind, block_rows(where)],
                in_recv.at[kind, where],
            ).start()

            def one(step, carry):
                target = lax.rem(me + step, lower)
                pltpu.make_async_remote_copy(
                    src_ref=staged.at[kind, target + lower, part_rows(0)],
                    dst_ref=full.at[kind, block_rows(where)],
                    send_sem=low_send.at[kind, step],
                    recv_sem=in_recv.at[kind, where],
                    device_id={"ctx": target},
                    device_id_type=pl.DeviceIdType.MESH,
                ).start()
                return carry

            lax.fori_loop(1, lower, one, 0)

        for head in range(helpers):
            held = staged.at[kind, head, part_rows(0)]
            place = full.at[kind, block_rows(where)]

            def act():
                send_piece(
                    held, place, lower + head, help_send.at[kind, head], in_recv.at[kind, where]
                )

            unless(low if kind in (QUERY, GRAD) else None, act)

    def wait_in(kind, block):
        def one(index, carry):
            held = full.at[kind, block_rows(index)]
            pltpu.make_async_copy(held, held, in_recv.at[kind, index]).wait()
            return carry

        lax.fori_loop(block * group, (block + 1) * group, one, 0)

    def send_piece(held, place, owner, send_sem, recv_sem):
        @pl.when(owner == me)
        def _():
            pltpu.make_async_copy(held, place, recv_sem).start()

        @pl.when(owner != me)
        def _():
            pltpu.make_async_remote_copy(
                src_ref=held,
                dst_ref=place,
                send_sem=send_sem,
                recv_sem=recv_sem,
                device_id={"ctx": owner},
                device_id_type=pl.DeviceIdType.MESH,
            ).start()

    def send_out(kind, block):
        for index in range(block * group, (block + 1) * group):
            part = 0 if index < shards else 1
            owner = index if part == 0 else 2 * shards - 1 - index
            send_piece(
                ready.at[kind, pl.ds(index * half, half)],
                out_ref.at[kind, me, part_rows(part)],
                owner,
                out_send.at[kind, index],
                out_recv.at[kind, part, me],
            )

    def send_more(kind, block, head):
        for step in range(group):
            owner = (block - blocks) * group + step
            held = ready.at[kind, pl.ds((2 * shards + owner) * half, half)]
            if kind in (OUT, DQ):
                place = out_ref.at[kind, head, part_rows(0)]
                recv_sem = out_recv.at[kind, 0, head]
            else:
                place = more_ref.at[kind - DK, me]
                recv_sem = more_recv.at[kind - DK, me]
            send_piece(held, place, owner, more_send.at[kind, owner], recv_sem)

    stage(KEY)
    pl.semaphore_wait(barrier, shards - 1)
    send_in(KEY, 0)
    stage(QUERY)
    send_in(QUERY, 0)
    stage(VALUE)
    send_in(VALUE, 0)
    for kind in (KEY, QUERY, VALUE):
        send_low(kind)
    stage(GRAD)

    docs = doc_ref[...].astype(jnp.float32).reshape(1, -1)
    for block in range(blocks):
        piece = docs[:, block * size : (block + 1) * size]
        doc_col[block] = jnp.broadcast_to(piece, (128, size)).T

    for kind in (KEY, QUERY, VALUE):
        sent_in(kind, 0)
        send_in(kind, 1)

    def rows_of(block):
        return pl.ds(block * size, size)

    def turn_keys(block):
        value_t[block] = full[VALUE, rows_of(block)].astype(jnp.float32).T.astype(jnp.bfloat16)
        key_t[block] = full[KEY, rows_of(block)].astype(jnp.float32).T.astype(jnp.bfloat16)

    def send_block(kind, block, head):
        if block >= blocks:
            send_more(kind, block, head)
        else:
            send_out(kind, block)

    def keys_of(block):
        return list(range(block, blocks - 1 if block >= blocks else -1, -1))

    def forward(block, head=None):
        keys = keys_of(block)
        for other in keys[1:]:
            if block >= blocks:
                wait_in(KEY, other)
                wait_in(VALUE, other)
                turn_keys(other)
        wait_in(KEY, block)
        wait_in(QUERY, block)
        queries = full[QUERY, rows_of(block)]
        at = block % blocks * size
        query_doc = docs[:, at : at + size]
        largest = None
        for other in keys:
            scores = nt_dot(full[KEY, rows_of(other)], queries)
            key_doc = jnp.concatenate([doc_col[other % blocks]] * (size // 128), axis=1)
            seen = key_doc == query_doc
            if other == block:
                key_at = lax.broadcasted_iota(jnp.int32, (size, size), 0)
                query_at = lax.broadcasted_iota(jnp.int32, (size, size), 1)
                seen = seen & (key_at <= query_at)
            scores = jnp.where(seen, scores, -1e30)
            score_buf[other % blocks] = scores
            top = jnp.max(scores, axis=0, keepdims=True)
            largest = top if largest is None else jnp.maximum(largest, top)
        total = jnp.zeros((1, size), jnp.float32)
        for other in keys:
            weights = jnp.exp2((score_buf[other % blocks] - largest) * (scaling * LOG2E))
            score_buf[other % blocks] = weights
            total = total + jnp.sum(weights, axis=0, keepdims=True)
        inverse = 1.0 / total
        wait_in(VALUE, block)
        turn_keys(block)
        accum = jnp.zeros((head_size, size), jnp.float32)
        for other in keys:
            probs = (score_buf[other % blocks] * inverse).astype(jnp.bfloat16)
            prob_buf[block, other % blocks] = probs
            accum = accum + jnp.dot(value_t[other], probs, preferred_element_type=jnp.float32)
        rounded = accum.astype(jnp.bfloat16).astype(jnp.float32)
        out_t[block] = rounded
        ready[OUT, rows_of(block)] = rounded.T.astype(jnp.bfloat16)
        send_block(OUT, block, head)

    def backward(block, head=None):
        keys = keys_of(block)
        wait_in(GRAD, block)
        queries = full[QUERY, rows_of(block)]
        grads = full[GRAD, rows_of(block)]
        delta = jnp.sum(grads.astype(jnp.float32).T * out_t[block], axis=0, keepdims=True)
        accum = jnp.zeros((head_size, size), jnp.float32)
        for other in keys:
            probs = prob_buf[block, other % blocks]
            dprobs = nt_dot(full[VALUE, rows_of(other)], grads)
            dscores = (probs.astype(jnp.float32) * (dprobs - delta)).astype(jnp.bfloat16)
            value_part = jnp.dot(probs, grads, preferred_element_type=jnp.float32)
            key_part = jnp.dot(dscores, queries, preferred_element_type=jnp.float32)
            if block < blocks - 1:
                value_part = value_part + value_acc[other]
                key_part = key_part + key_acc[other]
            if block >= blocks:
                finish_keys(other, value_part, key_part, head)
            elif other < block:
                value_acc[other] = value_part
                key_acc[other] = key_part
            else:
                finish_keys(block, value_part, key_part, head)
            accum = accum + jnp.dot(key_t[other], dscores, preferred_element_type=jnp.float32)
        ready[DQ, rows_of(block)] = (scaling * accum).T.astype(jnp.bfloat16)
        send_block(DQ, block, head)

    def finish_keys(block, value_part, key_part, head=None):
        ready[DV, rows_of(block)] = value_part.astype(jnp.bfloat16)
        send_block(DV, block, head)
        ready[DK, rows_of(block)] = (scaling * key_part).astype(jnp.bfloat16)
        send_block(DK, block, head)

    def keys_alone(block):
        wait_in(KEY, block)
        wait_in(VALUE, block)
        turn_keys(block)

    def either(condition, first, second):
        pl.when(condition)(first)
        pl.when(jnp.logical_not(condition))(second)

    spare = more_ref.at[:, pl.ds(0, lower)]

    def fill_zeros():
        zeros[...] = jnp.zeros_like(zeros)
        pltpu.make_async_copy(zeros, spare, zero_sem).start()
        keys_alone(0)

    either(low, lambda: forward(0), fill_zeros)
    either(helped, lambda: keys_alone(1), lambda: forward(1))
    for kind, part in ((KEY, 1), (QUERY, 0)):
        sent_in(kind, 1)
        send_in(GRAD, part)
    send_low(GRAD)
    pl.when(low)(lambda: forward(blocks, me + lower))
    pl.when(helping)(lambda: forward(blocks + 1, me - lower))
    for block in range(2, blocks):
        forward(block)

    for block in reversed(range(2, blocks)):
        backward(block)

    either(helped, lambda: finish_keys(1, value_acc[1], key_acc[1]), lambda: backward(1))

    def upper_end():
        finish_keys(0, value_acc[0], key_acc[0])
        pltpu.make_async_copy(zeros, spare, zero_sem).wait()

    either(low, lambda: backward(0), upper_end)
    pl.when(low)(lambda: backward(blocks, me + lower))
    pl.when(helping)(lambda: backward(blocks + 1, me - lower))

    for kind, part in ((VALUE, 1), (GRAD, 1), (GRAD, 0)):
        sent_in(kind, part)

    @pl.when(low)
    def _():
        def drain_low(step, carry):
            for kind in range(4):
                left = staged.at[kind, lax.rem(me + step, lower) + lower, part_rows(0)]
                pltpu.make_async_copy(left, left, low_send.at[kind, step]).wait()
            return carry

        lax.fori_loop(1, lower, drain_low, 0)

        def drain_more(index, carry):
            @pl.when(index != me)
            def _():
                for kind in range(4):
                    left = ready.at[kind, block_rows(2 * shards + index)]
                    pltpu.make_async_copy(left, left, more_send.at[kind, index]).wait()

            return carry

        lax.fori_loop(0, lower, drain_more, 0)

    @pl.when(helping)
    def _():
        def drain_more(index, carry):
            @pl.when(index != me)
            def _():
                for kind in range(4):

                    def act():
                        left = ready.at[kind, block_rows(2 * shards + index)]
                        pltpu.make_async_copy(left, left, more_send.at[kind, index]).wait()

                    unless(index < lower if kind in (OUT, DQ) else None, act)

            return carry

        lax.fori_loop(0, shards, drain_more, 0)

    for head in range(helpers):

        @pl.when(me != lower + head)
        def _():
            for kind in range(4):

                def act():
                    left = staged.at[kind, head, part_rows(0)]
                    pltpu.make_async_copy(left, left, help_send.at[kind, head]).wait()

                unless(low if kind in (QUERY, GRAD) else None, act)

    def collect_more(source, carry):
        for kind in range(2):
            place = more_ref.at[kind, source]
            pltpu.make_async_copy(place, place, more_recv.at[kind, source]).wait()
        return carry

    @pl.when(low)
    def _():
        lax.fori_loop(0, lower, collect_more, 0)

    lax.fori_loop(lower, lower + helpers, collect_more, 0)

    def drain_out(index, carry):
        owner = jnp.where(index < shards, index, 2 * shards - 1 - index)

        @pl.when(owner != me)
        def _():
            for kind in range(4):

                def act():
                    left = ready.at[kind, block_rows(index)]
                    pltpu.make_async_copy(left, left, out_send.at[kind, index]).wait()

                kept = None
                if kind in (OUT, DQ):
                    kept = (jnp.logical_not(low) & (index < lower)) | (
                        helped & (index >= lower) & (index < shards)
                    )
                unless(kept, act)

        return carry

    lax.fori_loop(0, 2 * shards, drain_out, 0)

    def collect(source, carry):
        for kind in range(4):
            for part in range(2):
                place = out_ref.at[kind, source, part_rows(part)]
                pltpu.make_async_copy(place, place, out_recv.at[kind, part, source]).wait()
        return carry

    lax.fori_loop(0, shards, collect, 0)


def rows_kernel(
    heads_ref, more_ref, out_a, out_b, out_c, out_d, held, more, wide, turned, in_sem, out_sem
):
    heads, rows, head_size = held.shape[1:]
    outs = (out_a, out_b, out_c, out_d)
    reads = [
        pltpu.make_async_copy(heads_ref.at[kind], held.at[kind], in_sem.at[kind])
        for kind in range(4)
    ]
    writes = [
        pltpu.make_async_copy(turned.at[kind], outs[kind], out_sem.at[kind]) for kind in range(4)
    ]
    half = more.shape[2]
    late = pltpu.make_async_copy(more_ref, more, in_sem.at[4])
    late.start()
    for read in reads:
        read.start()
    for kind in range(4):
        reads[kind].wait()
        if kind == DK:
            late.wait()
        for head in range(heads):
            wide[pl.ds(head, rows, stride=heads), :] = held[kind, head].astype(jnp.float32)
        if kind in (DK, DV):
            for slot in range(more.shape[1]):
                first = pl.ds((slot + heads // 2) % heads, half, stride=heads)
                wide[first, :] = wide[first, :] + more[kind - DK, slot].astype(jnp.float32)
        turned[kind] = wide[...].reshape(rows, heads, head_size).astype(jnp.bfloat16)
        writes[kind].start()
    for write in writes:
        write.wait()


def by_heads(queries, key_vecs, value_vecs, out_grad, doc_ids):
    shard_rows, head_count, head_size = queries.shape
    shards = lax.axis_size("ctx")
    half = shard_rows // 2
    tokens = shard_rows * shards
    group = 4
    size = group * half
    blocks = tokens // size
    slots = shards // 2 + shards // 4
    bf16, f32 = jnp.bfloat16, jnp.float32
    vmem = pl.BlockSpec(memory_space=pltpu.VMEM)
    flops = 7 * tokens * tokens * head_size
    results, more = pl.pallas_call(
        functools.partial(head_kernel, shards, half, group),
        out_shape=[
            jax.ShapeDtypeStruct((4, shards, shard_rows, head_size), bf16),
            jax.ShapeDtypeStruct((2, slots, half, head_size), bf16),
        ],
        in_specs=[pl.BlockSpec(memory_space=pltpu.HBM)] * 4 + [vmem],
        out_specs=[pl.BlockSpec(memory_space=pl.ANY)] * 2,
        scratch_shapes=[
            pltpu.VMEM((4, shard_rows, shards, head_size), bf16),
            pltpu.VMEM((4, shards, shard_rows, head_size), bf16),
            pltpu.VMEM((tokens, head_size), f32),
            pltpu.VMEM((4, tokens + 2 * size, head_size), bf16),
            pltpu.VMEM((4, tokens + 2 * size, head_size), bf16),
            pltpu.VMEM((2, shards // 2, half, head_size), bf16),
            pltpu.VMEM((blocks, size, 128), f32),
            pltpu.VMEM((blocks + 2, head_size, size), bf16),
            pltpu.VMEM((blocks + 2, head_size, size), bf16),
            pltpu.VMEM((blocks + 2, head_size, size), f32),
            pltpu.VMEM((blocks, size, size), f32),
            pltpu.VMEM((blocks + 2, blocks, size, size), bf16),
            pltpu.VMEM((blocks, size, head_size), f32),
            pltpu.VMEM((blocks, size, head_size), f32),
            pltpu.SemaphoreType.DMA((4, 2, shards)),
            pltpu.SemaphoreType.DMA((4, 3 * shards)),
            pltpu.SemaphoreType.DMA((4, 2 * shards)),
            pltpu.SemaphoreType.DMA((4, 2, shards)),
            pltpu.SemaphoreType.DMA((4,)),
            pltpu.SemaphoreType.DMA((4, shards // 2)),
            pltpu.SemaphoreType.DMA((4, shards)),
            pltpu.SemaphoreType.DMA((2, slots)),
            pltpu.SemaphoreType.DMA((4, shards // 4)),
            pltpu.SemaphoreType.DMA,
        ],
        compiler_params=pltpu.CompilerParams(
            collective_id=0, has_side_effects=True, vmem_limit_bytes=VMEM_BYTES
        ),
        cost_estimate=pl.CostEstimate(
            flops=flops, bytes_accessed=8 * queries.size * 2, transcendentals=tokens * tokens // 2
        ),
    )(key_vecs, queries, value_vecs, out_grad, doc_ids)
    rows_first = jax.ShapeDtypeStruct((shard_rows, shards, head_size), bf16)
    return pl.pallas_call(
        rows_kernel,
        out_shape=[rows_first] * 4,
        in_specs=[pl.BlockSpec(memory_space=pl.ANY)] * 2,
        out_specs=[pl.BlockSpec(memory_space=pl.ANY)] * 4,
        scratch_shapes=[
            pltpu.VMEM((4, shards, shard_rows, head_size), bf16),
            pltpu.VMEM((2, slots, half, head_size), bf16),
            pltpu.VMEM((shard_rows * shards, head_size), f32),
            pltpu.VMEM((4, shard_rows, shards, head_size), bf16),
            pltpu.SemaphoreType.DMA((5,)),
            pltpu.SemaphoreType.DMA((4,)),
        ],
        compiler_params=pltpu.CompilerParams(vmem_limit_bytes=VMEM_BYTES),
        cost_estimate=pl.CostEstimate(
            flops=0, bytes_accessed=16 * queries.size, transcendentals=0
        ),
    )(results, more)


def on_device(queries, key_vecs, value_vecs, out_grad, doc_ids):
    shard_rows, head_count, head_size = queries.shape
    fits = (
        head_count == lax.axis_size("ctx")
        and head_count == 8
        and shard_rows % 32 == 0
        and (2 * shard_rows) % 128 == 0
        and head_size == 128
    )
    attend = by_heads if fits else gathered
    return attend(queries, key_vecs, value_vecs, out_grad, doc_ids)


def solution(mesh):
    return jax.shard_map(
        on_device,
        mesh=mesh,
        in_specs=(
            P(("grp", "ctx"), "head", None),
            P(("grp", "ctx"), "head", None),
            P(("grp", "ctx"), "head", None),
            P(("grp", "ctx"), "head", None),
            P("grp"),
        ),
        out_specs=(
            P(("grp", "ctx"), "head", None),
            P(("grp", "ctx"), "head", None),
            P(("grp", "ctx"), "head", None),
            P(("grp", "ctx"), "head", None),
        ),
        check_vma=False,
    )
```

```python
import functools

import jax
import jax.numpy as jnp
from jax import lax
from jax.experimental import pallas as pl
from jax.experimental.pallas import tpu as pltpu
from jax.sharding import PartitionSpec as P


def block_length(shard_rows, shard_count):
    factor = 1
    while factor * shard_rows < 512 and shard_count % (factor * 2) == 0:
        factor = factor * 2
    return factor * shard_rows


def stored_position(rows, shard_rows, shard_count):
    half_rows = shard_rows // 2
    shard = rows // shard_rows
    within = rows % shard_rows
    return jnp.where(
        within < half_rows,
        shard * half_rows + within,
        (2 * shard_count - 1 - shard) * half_rows + within - half_rows,
    )


def score_block(query_blk, query_pos, query_doc, key_blk, key_pos, key_doc, scaling):
    scores = (
        jnp.einsum("qhd,khd->hqk", query_blk, key_blk, preferred_element_type=jnp.float32) * scaling
    )
    allowed = (key_doc[None, :] == query_doc[:, None]) & (key_pos[None, :] <= query_pos[:, None])
    return (scores, allowed[None])


def probs_of(scores, allowed, lse):
    return jnp.where(allowed, jnp.exp(scores - lse[:, :, None]), 0.0).astype(jnp.bfloat16)


def dscores_of(probs, grad_blk, value_blk, delta):
    dprobs = jnp.einsum("qhd,khd->hqk", grad_blk, value_blk, preferred_element_type=jnp.float32)
    return (probs.astype(jnp.float32) * (dprobs - delta[:, :, None])).astype(jnp.bfloat16)


def gathered(queries, key_vecs, value_vecs, out_grad, doc_ids):
    shard_rows = queries.shape[0]
    head_count = queries.shape[1]
    head_size = queries.shape[2]
    scaling = head_size ** (-0.5)
    shard_count = lax.axis_size("ctx")
    shard_index = lax.axis_index("ctx")
    own_start = shard_index * shard_rows

    def positions(start, length):
        return stored_position(start + jnp.arange(length, dtype=jnp.int32), shard_rows, shard_count)

    own_pos = positions(own_start, shard_rows)
    own_doc = jnp.take(doc_ids, own_pos)
    keys_all, values_all = (
        lax.all_gather(key_vecs, "ctx", axis=0, tiled=True),
        lax.all_gather(value_vecs, "ctx", axis=0, tiled=True),
    )
    block = block_length(shard_rows, shard_count)
    block_count = keys_all.shape[0] // block

    def key_slices(start, length):
        key_blk = lax.dynamic_slice_in_dim(keys_all, start, length, 0)
        value_blk = lax.dynamic_slice_in_dim(values_all, start, length, 0)
        key_pos = positions(start, length)
        key_doc = jnp.take(doc_ids, key_pos)
        return (key_blk, value_blk, key_pos, key_doc)

    def stat_step(index, carry):
        running, total = carry
        key_blk, value_blk, key_pos, key_doc = key_slices(index * block, block)
        scores, allowed = score_block(queries, own_pos, own_doc, key_blk, key_pos, key_doc, scaling)
        newmax = jnp.maximum(running, jnp.max(jnp.where(allowed, scores, -1e30), axis=-1))
        total = total * jnp.exp(running - newmax) + jnp.sum(
            jnp.where(allowed, jnp.exp(scores - newmax[:, :, None]), 0.0), axis=-1
        )
        return (newmax, total)

    start_max = jnp.full((head_count, shard_rows), -1e30, jnp.float32)
    start_sum = jnp.zeros((head_count, shard_rows), jnp.float32)
    running, total = lax.fori_loop(0, block_count, stat_step, (start_max, start_sum))
    lse = running + jnp.log(total)

    def out_step(index, accum):
        key_blk, value_blk, key_pos, key_doc = key_slices(index * block, block)
        scores, allowed = score_block(queries, own_pos, own_doc, key_blk, key_pos, key_doc, scaling)
        probs = probs_of(scores, allowed, lse)
        return accum + jnp.einsum(
            "hqk,khd->qhd", probs, value_blk, preferred_element_type=jnp.float32
        )

    zero_rows = jnp.zeros((shard_rows, head_count, head_size), jnp.float32)
    attn_out = lax.fori_loop(0, block_count, out_step, zero_rows).astype(jnp.bfloat16)
    delta_rows = jnp.sum(out_grad.astype(jnp.float32) * attn_out.astype(jnp.float32), axis=-1)
    delta = delta_rows.T

    def query_step(index, accum):
        key_blk, value_blk, key_pos, key_doc = key_slices(index * block, block)
        scores, allowed = score_block(queries, own_pos, own_doc, key_blk, key_pos, key_doc, scaling)
        probs = probs_of(scores, allowed, lse)
        dscores = dscores_of(probs, out_grad, value_blk, delta)
        return accum + jnp.einsum(
            "hqk,khd->qhd", dscores, key_blk, preferred_element_type=jnp.float32
        )

    query_grad = (scaling * lax.fori_loop(0, block_count, query_step, zero_rows)).astype(
        jnp.bfloat16
    )
    lse_all, delta_all = (
        lax.all_gather(lse.T, "ctx", axis=0, tiled=True),
        lax.all_gather(delta_rows, "ctx", axis=0, tiled=True),
    )
    query_blk = lax.all_gather(queries, "ctx", axis=0, tiled=True)
    grad_blk = lax.all_gather(out_grad, "ctx", axis=0, tiled=True)
    length = query_blk.shape[0]
    query_pos = positions(jnp.int32(0), length)
    query_doc = jnp.take(doc_ids, query_pos)
    lse_blk = lse_all.T
    delta_blk = delta_all.T
    scores, allowed = score_block(
        query_blk, query_pos, query_doc, key_vecs, own_pos, own_doc, scaling
    )
    probs = probs_of(scores, allowed, lse_blk)
    dscores = dscores_of(probs, grad_blk, value_vecs, delta_blk)
    key_accum = scaling * jnp.einsum(
        "hqk,qhd->khd", dscores, query_blk, preferred_element_type=jnp.float32
    )
    value_accum = jnp.einsum("hqk,qhd->khd", probs, grad_blk, preferred_element_type=jnp.float32)
    key_grad = key_accum.astype(jnp.bfloat16)
    value_grad = value_accum.astype(jnp.bfloat16)
    return (attn_out, query_grad, key_grad, value_grad)


KEY, QUERY, VALUE, GRAD = 0, 1, 2, 3
OUT, DQ, DK, DV = 0, 1, 2, 3
VMEM_BYTES = 62 * 1024 * 1024 + 600 * 1024
LOG2E = 1.4426950408889634


def nt_dot(a, b):
    return lax.dot_general(a, b, (((1,), (1,)), ((), ())), preferred_element_type=jnp.float32)


def head_kernel(
    shards,
    half,
    group,
    key_ref,
    query_ref,
    value_ref,
    grad_ref,
    doc_ref,
    out_ref,
    more_ref,
    fetched,
    staged,
    wide,
    full,
    ready,
    zeros,
    doc_col,
    key_t,
    value_t,
    out_t,
    score_buf,
    prob_buf,
    key_acc,
    value_acc,
    query_acc,
    deltas,
    in_send,
    in_recv,
    out_send,
    out_recv,
    fetch_sem,
    low_send,
    more_send,
    more_recv,
    help_send,
    zero_sem,
):
    me = lax.axis_index("ctx")
    lower = shards // 2
    low = me < lower
    helpers = lower // 2
    helped = me < helpers
    helping = (me >= lower) & (me < lower + helpers)
    size = half * group
    blocks = 2 * shards // group
    head_size = full.shape[-1]
    scaling = head_size ** (-0.5)

    fetches = [
        pltpu.make_async_copy(ref, fetched.at[kind], fetch_sem.at[kind])
        for kind, ref in ((KEY, key_ref), (QUERY, query_ref), (VALUE, value_ref), (GRAD, grad_ref))
    ]
    for fetch in fetches:
        fetch.start()

    barrier = pltpu.get_barrier_semaphore()

    def greet(step, carry):
        pl.semaphore_signal(
            barrier,
            inc=1,
            device_id={"ctx": lax.rem(me + step, shards)},
            device_id_type=pl.DeviceIdType.MESH,
        )
        return carry

    lax.fori_loop(1, shards, greet, 0)

    def stage(kind):
        fetches[kind].wait()
        rows = fetched.shape[1]
        wide[...] = fetched[kind].astype(jnp.float32).reshape(rows * shards, head_size)
        for head in range(shards):
            staged[kind, head] = wide[pl.ds(head, rows, stride=shards), :].astype(jnp.bfloat16)

    def part_rows(part):
        return pl.ds(part * half, half)

    def block_rows(index):
        return pl.ds(pl.multiple_of(index * half, half), half)

    def position(part):
        return me if part == 0 else 2 * shards - 1 - me

    def far_first(step):
        return lax.rem(step + shards // 2 - 2, shards - 1) + 1

    def diverted(kind, part, target):
        if part == 1 or kind in (KEY, VALUE):
            return None
        return (low & (target >= lower)) | ((me >= lower) & (target < helpers))

    def unless(skip, act):
        if skip is None:
            act()
        else:
            pl.when(jnp.logical_not(skip))(act)

    def sent_in(kind, part):
        def one(step, carry):
            target = lax.rem(me + far_first(step), shards)

            def act():
                left = staged.at[kind, target, part_rows(part)]
                pltpu.make_async_copy(left, left, in_send.at[kind, part, step]).wait()

            unless(diverted(kind, part, target), act)
            return carry

        lax.fori_loop(1, shards, one, 0)

    def send_in(kind, part):
        where = position(part)
        pltpu.make_async_copy(
            staged.at[kind, me, part_rows(part)],
            full.at[kind, block_rows(where)],
            in_recv.at[kind, where],
        ).start()

        def one(step, carry):
            target = lax.rem(me + far_first(step), shards)

            def act():
                pltpu.make_async_remote_copy(
                    src_ref=staged.at[kind, target, part_rows(part)],
                    dst_ref=full.at[kind, block_rows(where)],
                    send_sem=in_send.at[kind, part, step],
                    recv_sem=in_recv.at[kind, where],
                    device_id={"ctx": target},
                    device_id_type=pl.DeviceIdType.MESH,
                ).start()

            unless(diverted(kind, part, target), act)
            return carry

        lax.fori_loop(1, shards, one, 0)

    def send_low(kind):
        where = 2 * shards + me

        @pl.when(low)
        def _():
            pltpu.make_async_copy(
                staged.at[kind, me + lower, part_rows(0)],
                full.at[kind, block_rows(where)],
                in_recv.at[kind, where],
            ).start()

            def one(step, carry):
                target = lax.rem(me + step, lower)
                pltpu.make_async_remote_copy(
                    src_ref=staged.at[kind, target + lower, part_rows(0)],
                    dst_ref=full.at[kind, block_rows(where)],
                    send_sem=low_send.at[kind, step],
                    recv_sem=in_recv.at[kind, where],
                    device_id={"ctx": target},
                    device_id_type=pl.DeviceIdType.MESH,
                ).start()
                return carry

            lax.fori_loop(1, lower, one, 0)

        for head in range(helpers):
            held = staged.at[kind, head, part_rows(0)]
            place = full.at[kind, block_rows(where)]

            def act():
                send_piece(
                    held, place, lower + head, help_send.at[kind, head], in_recv.at[kind, where]
                )

            unless(low if kind in (QUERY, GRAD) else None, act)

    def wait_in(kind, block):
        def one(index, carry):
            held = full.at[kind, block_rows(index)]
            pltpu.make_async_copy(held, held, in_recv.at[kind, index]).wait()
            return carry

        lax.fori_loop(block * group, (block + 1) * group, one, 0)

    def send_piece(held, place, owner, send_sem, recv_sem):
        @pl.when(owner == me)
        def _():
            pltpu.make_async_copy(held, place, recv_sem).start()

        @pl.when(owner != me)
        def _():
            pltpu.make_async_remote_copy(
                src_ref=held,
                dst_ref=place,
                send_sem=send_sem,
                recv_sem=recv_sem,
                device_id={"ctx": owner},
                device_id_type=pl.DeviceIdType.MESH,
            ).start()

    def send_out(kind, block):
        for index in range(block * group, (block + 1) * group):
            part = 0 if index < shards else 1
            owner = index if part == 0 else 2 * shards - 1 - index
            send_piece(
                ready.at[kind, pl.ds(index * half, half)],
                out_ref.at[kind, me, part_rows(part)],
                owner,
                out_send.at[kind, index],
                out_recv.at[kind, part, me],
            )

    def send_more(kind, block, head):
        for step in range(group):
            owner = (block - blocks) * group + step
            held = ready.at[kind, pl.ds((2 * shards + owner) * half, half)]
            if kind in (OUT, DQ):
                place = out_ref.at[kind, head, part_rows(0)]
                recv_sem = out_recv.at[kind, 0, head]
            else:
                place = more_ref.at[kind - DK, me]
                recv_sem = more_recv.at[kind - DK, me]
            send_piece(held, place, owner, more_send.at[kind, owner], recv_sem)

    stage(KEY)
    pl.semaphore_wait(barrier, shards - 1)
    send_in(KEY, 0)
    stage(QUERY)
    send_in(QUERY, 0)
    stage(VALUE)
    send_in(VALUE, 0)
    for kind in (KEY, QUERY, VALUE):
        send_low(kind)
    stage(GRAD)

    docs = doc_ref[...].astype(jnp.float32).reshape(1, -1)
    for block in range(blocks):
        piece = docs[:, block * size : (block + 1) * size]
        doc_col[block] = jnp.broadcast_to(piece, (128, size)).T

    for kind in (KEY, QUERY, VALUE):
        sent_in(kind, 0)
        send_in(kind, 1)

    def rows_of(block):
        return pl.ds(block * size, size)

    def turn_keys(block):
        value_t[block] = full[VALUE, rows_of(block)].astype(jnp.float32).T.astype(jnp.bfloat16)
        key_t[block] = full[KEY, rows_of(block)].astype(jnp.float32).T.astype(jnp.bfloat16)

    def send_block(kind, block, head):
        if block >= blocks:
            send_more(kind, block, head)
        else:
            send_out(kind, block)

    def keys_of(block):
        return list(range(block, blocks - 1 if block >= blocks else -1, -1))

    def forward(block, head=None):
        keys = keys_of(block)
        for other in keys[1:]:
            if block >= blocks:
                wait_in(KEY, other)
                wait_in(VALUE, other)
                turn_keys(other)
        wait_in(KEY, block)
        wait_in(QUERY, block)
        queries = full[QUERY, rows_of(block)]
        at = block % blocks * size
        query_doc = docs[:, at : at + size]
        largest = None
        for other in keys:
            scores = nt_dot(full[KEY, rows_of(other)], queries)
            key_doc = jnp.concatenate([doc_col[other % blocks]] * (size // 128), axis=1)
            seen = key_doc == query_doc
            if other == block:
                key_at = lax.broadcasted_iota(jnp.int32, (size, size), 0)
                query_at = lax.broadcasted_iota(jnp.int32, (size, size), 1)
                seen = seen & (key_at <= query_at)
            scores = jnp.where(seen, scores, -1e30)
            score_buf[other % blocks] = scores
            top = jnp.max(scores, axis=0, keepdims=True)
            largest = top if largest is None else jnp.maximum(largest, top)
        total = jnp.zeros((1, size), jnp.float32)
        for other in keys:
            weights = jnp.exp2((score_buf[other % blocks] - largest) * (scaling * LOG2E))
            score_buf[other % blocks] = weights
            total = total + jnp.sum(weights, axis=0, keepdims=True)
        inverse = 1.0 / total
        wait_in(VALUE, block)
        turn_keys(block)
        accum = jnp.zeros((head_size, size), jnp.float32)
        for other in keys:
            probs = (score_buf[other % blocks] * inverse).astype(jnp.bfloat16)
            prob_buf[block, other % blocks] = probs
            accum = accum + jnp.dot(value_t[other], probs, preferred_element_type=jnp.float32)
        rounded = accum.astype(jnp.bfloat16).astype(jnp.float32)
        out_t[block] = rounded
        ready[OUT, rows_of(block)] = rounded.T.astype(jnp.bfloat16)
        send_block(OUT, block, head)

    def backward(pairs, new=(), done=(), head=None):
        for block, other in pairs:
            queries = full[QUERY, rows_of(block)]
            grads = full[GRAD, rows_of(block)]
            probs = prob_buf[block, other % blocks]
            dprobs = nt_dot(full[VALUE, rows_of(other)], grads)
            dscores = (probs.astype(jnp.float32) * (dprobs - deltas[block])).astype(jnp.bfloat16)
            value_part = jnp.dot(probs, grads, preferred_element_type=jnp.float32)
            key_part = jnp.dot(dscores, queries, preferred_element_type=jnp.float32)
            query_part = jnp.dot(key_t[other], dscores, preferred_element_type=jnp.float32)
            if ("k", block, other) not in new:
                value_part = value_part + value_acc[other]
                key_part = key_part + key_acc[other]
            if ("k", block, other) in done:
                finish_keys(other, value_part, key_part, head)
            else:
                value_acc[other] = value_part
                key_acc[other] = key_part
            if ("q", block, other) not in new:
                query_part = query_part + query_acc[block]
            if ("q", block, other) in done:
                ready[DQ, rows_of(block)] = (scaling * query_part).T.astype(jnp.bfloat16)
                send_block(DQ, block, head)
            else:
                query_acc[block] = query_part

    def ready_grads(block):
        wait_in(GRAD, block)
        grads = full[GRAD, rows_of(block)].astype(jnp.float32)
        deltas[block] = jnp.sum(grads.T * out_t[block], axis=0, keepdims=True)

    def plan(pairs):
        seen, new = set(), []
        for block, other in pairs:
            for name in (("q", block), ("k", other)):
                if name not in seen:
                    new.append((name[0], block, other))
                seen.add(name)
        return new

    def finish_keys(block, value_part, key_part, head=None):
        ready[DV, rows_of(block)] = value_part.astype(jnp.bfloat16)
        send_block(DV, block, head)
        ready[DK, rows_of(block)] = (scaling * key_part).astype(jnp.bfloat16)
        send_block(DK, block, head)

    def keys_alone(block):
        wait_in(KEY, block)
        wait_in(VALUE, block)
        turn_keys(block)

    def either(condition, first, second):
        pl.when(condition)(first)
        pl.when(jnp.logical_not(condition))(second)

    spare = more_ref.at[:, pl.ds(0, lower)]

    def fill_zeros():
        zeros[...] = jnp.zeros_like(zeros)
        pltpu.make_async_copy(zeros, spare, zero_sem).start()
        keys_alone(0)

    either(low, lambda: forward(0), fill_zeros)
    either(helped, lambda: keys_alone(1), lambda: forward(1))
    for kind, part in ((KEY, 1), (QUERY, 0)):
        sent_in(kind, 1)
        send_in(GRAD, part)
    send_low(GRAD)
    pl.when(low)(lambda: forward(blocks, me + lower))
    pl.when(helping)(lambda: forward(blocks + 1, me - lower))
    for block in range(2, blocks):
        forward(block)

    def lower_backward():
        late = blocks - 1
        first = [(late, 2), (2, 2), (2, 1), (2, 0), (late, 1)]
        backward(first, plan(first), [("k", 2, 2), ("q", 2, 0)])

        def second():
            ready_grads(1)
            backward(
                [(1, 1), (1, 0)], [("q", 1, 1)], [("k", 1, 1), ("q", 1, 0)]
            )

        either(helped, lambda: finish_keys(1, value_acc[1], key_acc[1]), second)
        home = [(late, 0), (late, late)]
        backward(home, [("k", late, late)], [("k", late, late), ("q", late, late)])
        ready_grads(0)
        backward([(0, 0)], [("q", 0, 0)], [("k", 0, 0), ("q", 0, 0)])
        extra = blocks
        ready_grads(extra)
        both = [("q", extra, extra), ("k", extra, extra)]
        backward([(extra, extra)], both, both, me + lower)

    def upper_backward():
        late = blocks - 1
        first = [(late, late), (late, 2), (late, 1), (late, 0), (2, 0)]
        backward(first, plan(first), [("k", late, late), ("q", late, 0)])
        ready_grads(1)
        backward([(1, 0)], [("q", 1, 0)], [("k", 1, 0)])

        @pl.when(helping)
        def _():
            extra = blocks + 1
            ready_grads(extra)
            pairs = [(extra, blocks), (extra, extra)]
            backward(
                pairs,
                plan(pairs),
                [("k", extra, blocks), ("k", extra, extra), ("q", extra, extra)],
                me - lower,
            )

        backward(
            [(2, 2), (2, 1), (1, 1)],
            [],
            [("k", 2, 2), ("q", 2, 1), ("k", 1, 1), ("q", 1, 1)],
        )
        pltpu.make_async_copy(zeros, spare, zero_sem).wait()

    for block in range(2, blocks):
        ready_grads(block)
    either(low, lower_backward, upper_backward)

    for kind, part in ((VALUE, 1), (GRAD, 1), (GRAD, 0)):
        sent_in(kind, part)

    @pl.when(low)
    def _():
        def drain_low(step, carry):
            for kind in range(4):
                left = staged.at[kind, lax.rem(me + step, lower) + lower, part_rows(0)]
                pltpu.make_async_copy(left, left, low_send.at[kind, step]).wait()
            return carry

        lax.fori_loop(1, lower, drain_low, 0)

        def drain_more(index, carry):
            @pl.when(index != me)
            def _():
                for kind in range(4):
                    left = ready.at[kind, block_rows(2 * shards + index)]
                    pltpu.make_async_copy(left, left, more_send.at[kind, index]).wait()

            return carry

        lax.fori_loop(0, lower, drain_more, 0)

    @pl.when(helping)
    def _():
        def drain_more(index, carry):
            @pl.when(index != me)
            def _():
                for kind in range(4):

                    def act():
                        left = ready.at[kind, block_rows(2 * shards + index)]
                        pltpu.make_async_copy(left, left, more_send.at[kind, index]).wait()

                    unless(index < lower if kind in (OUT, DQ) else None, act)

            return carry

        lax.fori_loop(0, shards, drain_more, 0)

    for head in range(helpers):

        @pl.when(me != lower + head)
        def _():
            for kind in range(4):

                def act():
                    left = staged.at[kind, head, part_rows(0)]
                    pltpu.make_async_copy(left, left, help_send.at[kind, head]).wait()

                unless(low if kind in (QUERY, GRAD) else None, act)

    def collect_more(source, carry):
        for kind in range(2):
            place = more_ref.at[kind, source]
            pltpu.make_async_copy(place, place, more_recv.at[kind, source]).wait()
        return carry

    @pl.when(low)
    def _():
        lax.fori_loop(0, lower, collect_more, 0)

    lax.fori_loop(lower, lower + helpers, collect_more, 0)

    def drain_out(index, carry):
        owner = jnp.where(index < shards, index, 2 * shards - 1 - index)

        @pl.when(owner != me)
        def _():
            for kind in range(4):

                def act():
                    left = ready.at[kind, block_rows(index)]
                    pltpu.make_async_copy(left, left, out_send.at[kind, index]).wait()

                kept = None
                if kind in (OUT, DQ):
                    kept = (jnp.logical_not(low) & (index < lower)) | (
                        helped & (index >= lower) & (index < shards)
                    )
                unless(kept, act)

        return carry

    lax.fori_loop(0, 2 * shards, drain_out, 0)

    def collect(source, carry):
        for kind in range(4):
            for part in range(2):
                place = out_ref.at[kind, source, part_rows(part)]
                pltpu.make_async_copy(place, place, out_recv.at[kind, part, source]).wait()
        return carry

    lax.fori_loop(0, shards, collect, 0)


def rows_kernel(
    heads_ref, more_ref, out_a, out_b, out_c, out_d, held, more, wide, turned, in_sem, out_sem
):
    heads, rows, head_size = held.shape[1:]
    outs = (out_a, out_b, out_c, out_d)
    reads = [
        pltpu.make_async_copy(heads_ref.at[kind], held.at[kind], in_sem.at[kind])
        for kind in range(4)
    ]
    writes = [
        pltpu.make_async_copy(turned.at[kind], outs[kind], out_sem.at[kind]) for kind in range(4)
    ]
    half = more.shape[2]
    late = pltpu.make_async_copy(more_ref, more, in_sem.at[4])
    late.start()
    for read in reads:
        read.start()
    for kind in range(4):
        reads[kind].wait()
        if kind == DK:
            late.wait()
        for head in range(heads):
            wide[pl.ds(head, rows, stride=heads), :] = held[kind, head].astype(jnp.float32)
        if kind in (DK, DV):
            for slot in range(more.shape[1]):
                first = pl.ds((slot + heads // 2) % heads, half, stride=heads)
                wide[first, :] = wide[first, :] + more[kind - DK, slot].astype(jnp.float32)
        turned[kind] = wide[...].reshape(rows, heads, head_size).astype(jnp.bfloat16)
        writes[kind].start()
    for write in writes:
        write.wait()


def by_heads(queries, key_vecs, value_vecs, out_grad, doc_ids):
    shard_rows, head_count, head_size = queries.shape
    shards = lax.axis_size("ctx")
    half = shard_rows // 2
    tokens = shard_rows * shards
    group = 4
    size = group * half
    blocks = tokens // size
    slots = shards // 2 + shards // 4
    bf16, f32 = jnp.bfloat16, jnp.float32
    vmem = pl.BlockSpec(memory_space=pltpu.VMEM)
    flops = 7 * tokens * tokens * head_size
    results, more = pl.pallas_call(
        functools.partial(head_kernel, shards, half, group),
        out_shape=[
            jax.ShapeDtypeStruct((4, shards, shard_rows, head_size), bf16),
            jax.ShapeDtypeStruct((2, slots, half, head_size), bf16),
        ],
        in_specs=[pl.BlockSpec(memory_space=pltpu.HBM)] * 4 + [vmem],
        out_specs=[pl.BlockSpec(memory_space=pl.ANY)] * 2,
        scratch_shapes=[
            pltpu.VMEM((4, shard_rows, shards, head_size), bf16),
            pltpu.VMEM((4, shards, shard_rows, head_size), bf16),
            pltpu.VMEM((tokens, head_size), f32),
            pltpu.VMEM((4, tokens + 2 * size, head_size), bf16),
            pltpu.VMEM((4, tokens + 2 * size, head_size), bf16),
            pltpu.VMEM((2, shards // 2, half, head_size), bf16),
            pltpu.VMEM((blocks, size, 128), f32),
            pltpu.VMEM((blocks + 2, head_size, size), bf16),
            pltpu.VMEM((blocks + 2, head_size, size), bf16),
            pltpu.VMEM((blocks + 2, head_size, size), f32),
            pltpu.VMEM((blocks, size, size), f32),
            pltpu.VMEM((blocks + 2, blocks, size, size), bf16),
            pltpu.VMEM((blocks + 2, size, head_size), f32),
            pltpu.VMEM((blocks + 2, size, head_size), f32),
            pltpu.VMEM((blocks + 2, head_size, size), f32),
            pltpu.VMEM((blocks + 2, 1, size), f32),
            pltpu.SemaphoreType.DMA((4, 2, shards)),
            pltpu.SemaphoreType.DMA((4, 3 * shards)),
            pltpu.SemaphoreType.DMA((4, 2 * shards)),
            pltpu.SemaphoreType.DMA((4, 2, shards)),
            pltpu.SemaphoreType.DMA((4,)),
            pltpu.SemaphoreType.DMA((4, shards // 2)),
            pltpu.SemaphoreType.DMA((4, shards)),
            pltpu.SemaphoreType.DMA((2, slots)),
            pltpu.SemaphoreType.DMA((4, shards // 4)),
            pltpu.SemaphoreType.DMA,
        ],
        compiler_params=pltpu.CompilerParams(
            collective_id=0, has_side_effects=True, vmem_limit_bytes=VMEM_BYTES
        ),
        cost_estimate=pl.CostEstimate(
            flops=flops, bytes_accessed=8 * queries.size * 2, transcendentals=tokens * tokens // 2
        ),
    )(key_vecs, queries, value_vecs, out_grad, doc_ids)
    rows_first = jax.ShapeDtypeStruct((shard_rows, shards, head_size), bf16)
    return pl.pallas_call(
        rows_kernel,
        out_shape=[rows_first] * 4,
        in_specs=[pl.BlockSpec(memory_space=pl.ANY)] * 2,
        out_specs=[pl.BlockSpec(memory_space=pl.ANY)] * 4,
        scratch_shapes=[
            pltpu.VMEM((4, shards, shard_rows, head_size), bf16),
            pltpu.VMEM((2, slots, half, head_size), bf16),
            pltpu.VMEM((shard_rows * shards, head_size), f32),
            pltpu.VMEM((4, shard_rows, shards, head_size), bf16),
            pltpu.SemaphoreType.DMA((5,)),
            pltpu.SemaphoreType.DMA((4,)),
        ],
        compiler_params=pltpu.CompilerParams(vmem_limit_bytes=VMEM_BYTES),
        cost_estimate=pl.CostEstimate(
            flops=0, bytes_accessed=16 * queries.size, transcendentals=0
        ),
    )(results, more)


def on_device(queries, key_vecs, value_vecs, out_grad, doc_ids):
    shard_rows, head_count, head_size = queries.shape
    fits = (
        head_count == lax.axis_size("ctx")
        and head_count == 8
        and shard_rows % 32 == 0
        and (2 * shard_rows) % 128 == 0
        and head_size == 128
    )
    attend = by_heads if fits else gathered
    return attend(queries, key_vecs, value_vecs, out_grad, doc_ids)


def solution(mesh):
    return jax.shard_map(
        on_device,
        mesh=mesh,
        in_specs=(
            P(("grp", "ctx"), "head", None),
            P(("grp", "ctx"), "head", None),
            P(("grp", "ctx"), "head", None),
            P(("grp", "ctx"), "head", None),
            P("grp"),
        ),
        out_specs=(
            P(("grp", "ctx"), "head", None),
            P(("grp", "ctx"), "head", None),
            P(("grp", "ctx"), "head", None),
            P(("grp", "ctx"), "head", None),
        ),
        check_vma=False,
    )
```

```python
import functools

import jax
import jax.numpy as jnp
from jax import lax
from jax.experimental import pallas as pl
from jax.experimental.pallas import tpu as pltpu
from jax.sharding import PartitionSpec as P


def block_length(shard_rows, shard_count):
    factor = 1
    while factor * shard_rows < 512 and shard_count % (factor * 2) == 0:
        factor = factor * 2
    return factor * shard_rows


def stored_position(rows, shard_rows, shard_count):
    half_rows = shard_rows // 2
    shard = rows // shard_rows
    within = rows % shard_rows
    return jnp.where(
        within < half_rows,
        shard * half_rows + within,
        (2 * shard_count - 1 - shard) * half_rows + within - half_rows,
    )


def score_block(query_blk, query_pos, query_doc, key_blk, key_pos, key_doc, scaling):
    scores = (
        jnp.einsum("qhd,khd->hqk", query_blk, key_blk, preferred_element_type=jnp.float32) * scaling
    )
    allowed = (key_doc[None, :] == query_doc[:, None]) & (key_pos[None, :] <= query_pos[:, None])
    return (scores, allowed[None])


def probs_of(scores, allowed, lse):
    return jnp.where(allowed, jnp.exp(scores - lse[:, :, None]), 0.0).astype(jnp.bfloat16)


def dscores_of(probs, grad_blk, value_blk, delta):
    dprobs = jnp.einsum("qhd,khd->hqk", grad_blk, value_blk, preferred_element_type=jnp.float32)
    return (probs.astype(jnp.float32) * (dprobs - delta[:, :, None])).astype(jnp.bfloat16)


def gathered(queries, key_vecs, value_vecs, out_grad, doc_ids):
    shard_rows = queries.shape[0]
    head_count = queries.shape[1]
    head_size = queries.shape[2]
    scaling = head_size ** (-0.5)
    shard_count = lax.axis_size("ctx")
    shard_index = lax.axis_index("ctx")
    own_start = shard_index * shard_rows

    def positions(start, length):
        return stored_position(start + jnp.arange(length, dtype=jnp.int32), shard_rows, shard_count)

    own_pos = positions(own_start, shard_rows)
    own_doc = jnp.take(doc_ids, own_pos)
    keys_all, values_all = (
        lax.all_gather(key_vecs, "ctx", axis=0, tiled=True),
        lax.all_gather(value_vecs, "ctx", axis=0, tiled=True),
    )
    block = block_length(shard_rows, shard_count)
    block_count = keys_all.shape[0] // block

    def key_slices(start, length):
        key_blk = lax.dynamic_slice_in_dim(keys_all, start, length, 0)
        value_blk = lax.dynamic_slice_in_dim(values_all, start, length, 0)
        key_pos = positions(start, length)
        key_doc = jnp.take(doc_ids, key_pos)
        return (key_blk, value_blk, key_pos, key_doc)

    def stat_step(index, carry):
        running, total = carry
        key_blk, value_blk, key_pos, key_doc = key_slices(index * block, block)
        scores, allowed = score_block(queries, own_pos, own_doc, key_blk, key_pos, key_doc, scaling)
        newmax = jnp.maximum(running, jnp.max(jnp.where(allowed, scores, -1e30), axis=-1))
        total = total * jnp.exp(running - newmax) + jnp.sum(
            jnp.where(allowed, jnp.exp(scores - newmax[:, :, None]), 0.0), axis=-1
        )
        return (newmax, total)

    start_max = jnp.full((head_count, shard_rows), -1e30, jnp.float32)
    start_sum = jnp.zeros((head_count, shard_rows), jnp.float32)
    running, total = lax.fori_loop(0, block_count, stat_step, (start_max, start_sum))
    lse = running + jnp.log(total)

    def out_step(index, accum):
        key_blk, value_blk, key_pos, key_doc = key_slices(index * block, block)
        scores, allowed = score_block(queries, own_pos, own_doc, key_blk, key_pos, key_doc, scaling)
        probs = probs_of(scores, allowed, lse)
        return accum + jnp.einsum(
            "hqk,khd->qhd", probs, value_blk, preferred_element_type=jnp.float32
        )

    zero_rows = jnp.zeros((shard_rows, head_count, head_size), jnp.float32)
    attn_out = lax.fori_loop(0, block_count, out_step, zero_rows).astype(jnp.bfloat16)
    delta_rows = jnp.sum(out_grad.astype(jnp.float32) * attn_out.astype(jnp.float32), axis=-1)
    delta = delta_rows.T

    def query_step(index, accum):
        key_blk, value_blk, key_pos, key_doc = key_slices(index * block, block)
        scores, allowed = score_block(queries, own_pos, own_doc, key_blk, key_pos, key_doc, scaling)
        probs = probs_of(scores, allowed, lse)
        dscores = dscores_of(probs, out_grad, value_blk, delta)
        return accum + jnp.einsum(
            "hqk,khd->qhd", dscores, key_blk, preferred_element_type=jnp.float32
        )

    query_grad = (scaling * lax.fori_loop(0, block_count, query_step, zero_rows)).astype(
        jnp.bfloat16
    )
    lse_all, delta_all = (
        lax.all_gather(lse.T, "ctx", axis=0, tiled=True),
        lax.all_gather(delta_rows, "ctx", axis=0, tiled=True),
    )
    query_blk = lax.all_gather(queries, "ctx", axis=0, tiled=True)
    grad_blk = lax.all_gather(out_grad, "ctx", axis=0, tiled=True)
    length = query_blk.shape[0]
    query_pos = positions(jnp.int32(0), length)
    query_doc = jnp.take(doc_ids, query_pos)
    lse_blk = lse_all.T
    delta_blk = delta_all.T
    scores, allowed = score_block(
        query_blk, query_pos, query_doc, key_vecs, own_pos, own_doc, scaling
    )
    probs = probs_of(scores, allowed, lse_blk)
    dscores = dscores_of(probs, grad_blk, value_vecs, delta_blk)
    key_accum = scaling * jnp.einsum(
        "hqk,qhd->khd", dscores, query_blk, preferred_element_type=jnp.float32
    )
    value_accum = jnp.einsum("hqk,qhd->khd", probs, grad_blk, preferred_element_type=jnp.float32)
    key_grad = key_accum.astype(jnp.bfloat16)
    value_grad = value_accum.astype(jnp.bfloat16)
    return (attn_out, query_grad, key_grad, value_grad)


KEY, QUERY, VALUE, GRAD = 0, 1, 2, 3
OUT, DQ, DK, DV = 0, 1, 2, 3
VMEM_BYTES = 62 * 1024 * 1024 + 600 * 1024
LOG2E = 1.4426950408889634


def nt_dot(a, b):
    return lax.dot_general(a, b, (((1,), (1,)), ((), ())), preferred_element_type=jnp.float32)


def head_kernel(
    shards,
    half,
    group,
    key_ref,
    query_ref,
    value_ref,
    grad_ref,
    doc_ref,
    out_ref,
    more_ref,
    fetched,
    staged,
    wide,
    full,
    ready,
    zeros,
    doc_col,
    key_t,
    value_t,
    out_t,
    score_buf,
    prob_buf,
    key_acc,
    value_acc,
    query_acc,
    deltas,
    in_send,
    in_recv,
    out_send,
    out_recv,
    fetch_sem,
    low_send,
    more_send,
    more_recv,
    help_send,
    zero_sem,
):
    me = lax.axis_index("ctx")
    lower = shards // 2
    low = me < lower
    helpers = lower // 2
    helped = me < helpers
    helping = (me >= lower) & (me < lower + helpers)
    size = half * group
    blocks = 2 * shards // group
    head_size = full.shape[-1]
    scaling = head_size ** (-0.5)

    fetches = [
        pltpu.make_async_copy(ref, fetched.at[kind], fetch_sem.at[kind])
        for kind, ref in ((KEY, key_ref), (QUERY, query_ref), (VALUE, value_ref), (GRAD, grad_ref))
    ]
    for fetch in fetches:
        fetch.start()

    barrier = pltpu.get_barrier_semaphore()

    def greet(step, carry):
        pl.semaphore_signal(
            barrier,
            inc=1,
            device_id={"ctx": lax.rem(me + step, shards)},
            device_id_type=pl.DeviceIdType.MESH,
        )
        return carry

    lax.fori_loop(1, shards, greet, 0)

    def stage(kind):
        fetches[kind].wait()
        rows = fetched.shape[1]
        wide[...] = fetched[kind].astype(jnp.float32).reshape(rows * shards, head_size)
        for head in range(shards):
            staged[kind, head] = wide[pl.ds(head, rows, stride=shards), :].astype(jnp.bfloat16)

    def part_rows(part):
        return pl.ds(part * half, half)

    def block_rows(index):
        return pl.ds(pl.multiple_of(index * half, half), half)

    def position(part):
        return me if part == 0 else 2 * shards - 1 - me

    def far_first(step):
        return lax.rem(step + shards // 2 - 2, shards - 1) + 1

    def diverted(kind, part, target):
        if part == 1 or kind in (KEY, VALUE):
            return None
        return (low & (target >= lower)) | ((me >= lower) & (target < helpers))

    def unless(skip, act):
        if skip is None:
            act()
        else:
            pl.when(jnp.logical_not(skip))(act)

    def sent_in(kind, part):
        def one(step, carry):
            target = lax.rem(me + far_first(step), shards)

            def act():
                left = staged.at[kind, target, part_rows(part)]
                pltpu.make_async_copy(left, left, in_send.at[kind, part, step]).wait()

            unless(diverted(kind, part, target), act)
            return carry

        lax.fori_loop(1, shards, one, 0)

    def send_in(kind, part):
        where = position(part)
        pltpu.make_async_copy(
            staged.at[kind, me, part_rows(part)],
            full.at[kind, block_rows(where)],
            in_recv.at[kind, where],
        ).start()

        def one(step, carry):
            target = lax.rem(me + far_first(step), shards)

            def act():
                pltpu.make_async_remote_copy(
                    src_ref=staged.at[kind, target, part_rows(part)],
                    dst_ref=full.at[kind, block_rows(where)],
                    send_sem=in_send.at[kind, part, step],
                    recv_sem=in_recv.at[kind, where],
                    device_id={"ctx": target},
                    device_id_type=pl.DeviceIdType.MESH,
                ).start()

            unless(diverted(kind, part, target), act)
            return carry

        lax.fori_loop(1, shards, one, 0)

    def send_low(kind):
        where = 2 * shards + me

        @pl.when(low)
        def _():
            pltpu.make_async_copy(
                staged.at[kind, me + lower, part_rows(0)],
                full.at[kind, block_rows(where)],
                in_recv.at[kind, where],
            ).start()

            def one(step, carry):
                target = lax.rem(me + step, lower)
                pltpu.make_async_remote_copy(
                    src_ref=staged.at[kind, target + lower, part_rows(0)],
                    dst_ref=full.at[kind, block_rows(where)],
                    send_sem=low_send.at[kind, step],
                    recv_sem=in_recv.at[kind, where],
                    device_id={"ctx": target},
                    device_id_type=pl.DeviceIdType.MESH,
                ).start()
                return carry

            lax.fori_loop(1, lower, one, 0)

        for head in range(helpers):
            held = staged.at[kind, head, part_rows(0)]
            place = full.at[kind, block_rows(where)]

            def act():
                send_piece(
                    held, place, lower + head, help_send.at[kind, head], in_recv.at[kind, where]
                )

            unless(low if kind in (QUERY, GRAD) else None, act)

    def wait_in(kind, block):
        def one(index, carry):
            held = full.at[kind, block_rows(index)]
            pltpu.make_async_copy(held, held, in_recv.at[kind, index]).wait()
            return carry

        lax.fori_loop(block * group, (block + 1) * group, one, 0)

    def send_piece(held, place, owner, send_sem, recv_sem):
        @pl.when(owner == me)
        def _():
            pltpu.make_async_copy(held, place, recv_sem).start()

        @pl.when(owner != me)
        def _():
            pltpu.make_async_remote_copy(
                src_ref=held,
                dst_ref=place,
                send_sem=send_sem,
                recv_sem=recv_sem,
                device_id={"ctx": owner},
                device_id_type=pl.DeviceIdType.MESH,
            ).start()

    def send_out(kind, block):
        for index in range(block * group, (block + 1) * group):
            part = 0 if index < shards else 1
            owner = index if part == 0 else 2 * shards - 1 - index
            send_piece(
                ready.at[kind, pl.ds(index * half, half)],
                out_ref.at[kind, me, part_rows(part)],
                owner,
                out_send.at[kind, index],
                out_recv.at[kind, part, me],
            )

    def send_more(kind, block, head):
        for step in range(group):
            owner = (block - blocks) * group + step
            held = ready.at[kind, pl.ds((2 * shards + owner) * half, half)]
            if kind in (OUT, DQ):
                place = out_ref.at[kind, head, part_rows(0)]
                recv_sem = out_recv.at[kind, 0, head]
            else:
                place = more_ref.at[kind - DK, me]
                recv_sem = more_recv.at[kind - DK, me]
            send_piece(held, place, owner, more_send.at[kind, owner], recv_sem)

    stage(KEY)
    pl.semaphore_wait(barrier, shards - 1)
    send_in(KEY, 0)
    stage(QUERY)
    send_in(QUERY, 0)
    stage(VALUE)
    send_in(VALUE, 0)
    for kind in (KEY, QUERY, VALUE):
        send_low(kind)
    stage(GRAD)
    send_low(GRAD)

    docs = doc_ref[...].astype(jnp.float32).reshape(1, -1)
    for block in range(blocks):
        piece = docs[:, block * size : (block + 1) * size]
        doc_col[block] = jnp.broadcast_to(piece, (128, size)).T

    for kind in (KEY, QUERY, VALUE):
        sent_in(kind, 0)
        send_in(kind, 1)

    def rows_of(block):
        return pl.ds(block * size, size)

    def turn_keys(block):
        value_t[block] = full[VALUE, rows_of(block)].astype(jnp.float32).T.astype(jnp.bfloat16)
        key_t[block] = full[KEY, rows_of(block)].astype(jnp.float32).T.astype(jnp.bfloat16)

    def send_block(kind, block, head):
        if block >= blocks:
            send_more(kind, block, head)
        else:
            send_out(kind, block)

    def keys_of(block):
        return list(range(block, blocks - 1 if block >= blocks else -1, -1))

    def forward(block, head=None):
        keys = keys_of(block)
        for other in keys[1:]:
            if block >= blocks:
                wait_in(KEY, other)
                wait_in(VALUE, other)
                turn_keys(other)
        wait_in(KEY, block)
        wait_in(QUERY, block)
        queries = full[QUERY, rows_of(block)]
        at = block % blocks * size
        query_doc = docs[:, at : at + size]
        largest = None
        for other in keys:
            scores = nt_dot(full[KEY, rows_of(other)], queries)
            key_doc = jnp.concatenate([doc_col[other % blocks]] * (size // 128), axis=1)
            seen = key_doc == query_doc
            if other == block:
                key_at = lax.broadcasted_iota(jnp.int32, (size, size), 0)
                query_at = lax.broadcasted_iota(jnp.int32, (size, size), 1)
                seen = seen & (key_at <= query_at)
            scores = jnp.where(seen, scores, -1e30)
            score_buf[other % blocks] = scores
            top = jnp.max(scores, axis=0, keepdims=True)
            largest = top if largest is None else jnp.maximum(largest, top)
        total = jnp.zeros((1, size), jnp.float32)
        for other in keys:
            weights = jnp.exp2((score_buf[other % blocks] - largest) * (scaling * LOG2E))
            score_buf[other % blocks] = weights
            total = total + jnp.sum(weights, axis=0, keepdims=True)
        inverse = 1.0 / total
        wait_in(VALUE, block)
        turn_keys(block)
        accum = jnp.zeros((head_size, size), jnp.float32)
        for other in keys:
            probs = (score_buf[other % blocks] * inverse).astype(jnp.bfloat16)
            prob_buf[block, other % blocks] = probs
            accum = accum + jnp.dot(value_t[other], probs, preferred_element_type=jnp.float32)
        rounded = accum.astype(jnp.bfloat16).astype(jnp.float32)
        out_t[block] = rounded
        ready[OUT, rows_of(block)] = rounded.T.astype(jnp.bfloat16)
        send_block(OUT, block, head)

    def backward(pairs, new=(), done=(), head=None):
        for block, other in pairs:
            queries = full[QUERY, rows_of(block)]
            grads = full[GRAD, rows_of(block)]
            probs = prob_buf[block, other % blocks]
            dprobs = nt_dot(full[VALUE, rows_of(other)], grads)
            dscores = (probs.astype(jnp.float32) * (dprobs - deltas[block])).astype(jnp.bfloat16)
            value_part = jnp.dot(probs, grads, preferred_element_type=jnp.float32)
            key_part = jnp.dot(dscores, queries, preferred_element_type=jnp.float32)
            query_part = jnp.dot(key_t[other], dscores, preferred_element_type=jnp.float32)
            if ("k", block, other) not in new:
                value_part = value_part + value_acc[other]
                key_part = key_part + key_acc[other]
            if ("k", block, other) in done:
                finish_keys(other, value_part, key_part, head)
            else:
                value_acc[other] = value_part
                key_acc[other] = key_part
            if ("q", block, other) not in new:
                query_part = query_part + query_acc[block]
            if ("q", block, other) in done:
                ready[DQ, rows_of(block)] = (scaling * query_part).T.astype(jnp.bfloat16)
                send_block(DQ, block, head)
            else:
                query_acc[block] = query_part

    def ready_grads(block):
        wait_in(GRAD, block)
        grads = full[GRAD, rows_of(block)].astype(jnp.float32)
        deltas[block] = jnp.sum(grads.T * out_t[block], axis=0, keepdims=True)

    def plan(pairs):
        seen, new = set(), []
        for block, other in pairs:
            for name in (("q", block), ("k", other)):
                if name not in seen:
                    new.append((name[0], block, other))
                seen.add(name)
        return new

    def finish_keys(block, value_part, key_part, head=None):
        ready[DV, rows_of(block)] = value_part.astype(jnp.bfloat16)
        send_block(DV, block, head)
        ready[DK, rows_of(block)] = (scaling * key_part).astype(jnp.bfloat16)
        send_block(DK, block, head)

    def keys_alone(block):
        wait_in(KEY, block)
        wait_in(VALUE, block)
        turn_keys(block)

    def either(condition, first, second):
        pl.when(condition)(first)
        pl.when(jnp.logical_not(condition))(second)

    spare = more_ref.at[:, pl.ds(0, lower)]

    def fill_zeros():
        zeros[...] = jnp.zeros_like(zeros)
        pltpu.make_async_copy(zeros, spare, zero_sem).start()
        keys_alone(0)

    either(low, lambda: forward(0), fill_zeros)
    either(helped, lambda: keys_alone(1), lambda: forward(1))
    for kind, part in ((KEY, 1), (QUERY, 0)):
        sent_in(kind, 1)
        send_in(GRAD, part)

    @pl.when(low)
    def _():
        extra = blocks
        forward(extra, me + lower)
        ready_grads(extra)
        both = [("q", extra, extra), ("k", extra, extra)]
        backward([(extra, extra)], both, both, me + lower)

    @pl.when(helping)
    def _():
        extra = blocks + 1
        forward(extra, me - lower)
        ready_grads(extra)
        pairs = [(extra, blocks), (extra, extra)]
        done = [("k", extra, blocks), ("k", extra, extra), ("q", extra, extra)]
        backward(pairs, plan(pairs), done, me - lower)

    for block in range(2, blocks):
        forward(block)

    def lower_backward():
        late = blocks - 1
        first = [(late, late), (late, 2), (2, 2), (2, 1), (2, 0), (late, 1), (late, 0)]
        done = [("k", late, late), ("k", 2, 2), ("q", 2, 0), ("q", late, 0)]
        backward(first, plan(first), done)

        def second():
            ready_grads(1)
            backward([(1, 1), (1, 0)], [("q", 1, 1)], [("k", 1, 1), ("q", 1, 0)])

        either(helped, lambda: finish_keys(1, value_acc[1], key_acc[1]), second)
        ready_grads(0)
        backward([(0, 0)], [("q", 0, 0)], [("k", 0, 0), ("q", 0, 0)])

    def upper_backward():
        late = blocks - 1
        first = [(late, late), (late, 2), (2, 2), (late, 1), (late, 0), (2, 1), (2, 0)]
        done = [("k", late, late), ("k", 2, 2), ("q", late, 0), ("q", 2, 0)]
        backward(first, plan(first), done)
        ready_grads(1)
        done = [("k", 1, 0), ("k", 1, 1), ("q", 1, 1)]
        backward([(1, 0), (1, 1)], [("q", 1, 0)], done)
        pltpu.make_async_copy(zeros, spare, zero_sem).wait()

    for block in range(2, blocks):
        ready_grads(block)
    either(low, lower_backward, upper_backward)

    for kind, part in ((VALUE, 1), (GRAD, 1), (GRAD, 0)):
        sent_in(kind, part)

    @pl.when(low)
    def _():
        def drain_low(step, carry):
            for kind in range(4):
                left = staged.at[kind, lax.rem(me + step, lower) + lower, part_rows(0)]
                pltpu.make_async_copy(left, left, low_send.at[kind, step]).wait()
            return carry

        lax.fori_loop(1, lower, drain_low, 0)

        def drain_more(index, carry):
            @pl.when(index != me)
            def _():
                for kind in range(4):
                    left = ready.at[kind, block_rows(2 * shards + index)]
                    pltpu.make_async_copy(left, left, more_send.at[kind, index]).wait()

            return carry

        lax.fori_loop(0, lower, drain_more, 0)

    @pl.when(helping)
    def _():
        def drain_more(index, carry):
            @pl.when(index != me)
            def _():
                for kind in range(4):

                    def act():
                        left = ready.at[kind, block_rows(2 * shards + index)]
                        pltpu.make_async_copy(left, left, more_send.at[kind, index]).wait()

                    unless(index < lower if kind in (OUT, DQ) else None, act)

            return carry

        lax.fori_loop(0, shards, drain_more, 0)

    for head in range(helpers):

        @pl.when(me != lower + head)
        def _():
            for kind in range(4):

                def act():
                    left = staged.at[kind, head, part_rows(0)]
                    pltpu.make_async_copy(left, left, help_send.at[kind, head]).wait()

                unless(low if kind in (QUERY, GRAD) else None, act)

    def collect_more(source, carry):
        for kind in range(2):
            place = more_ref.at[kind, source]
            pltpu.make_async_copy(place, place, more_recv.at[kind, source]).wait()
        return carry

    @pl.when(low)
    def _():
        lax.fori_loop(0, lower, collect_more, 0)

    lax.fori_loop(lower, lower + helpers, collect_more, 0)

    def drain_out(index, carry):
        owner = jnp.where(index < shards, index, 2 * shards - 1 - index)

        @pl.when(owner != me)
        def _():
            for kind in range(4):

                def act():
                    left = ready.at[kind, block_rows(index)]
                    pltpu.make_async_copy(left, left, out_send.at[kind, index]).wait()

                kept = None
                if kind in (OUT, DQ):
                    kept = (jnp.logical_not(low) & (index < lower)) | (
                        helped & (index >= lower) & (index < shards)
                    )
                unless(kept, act)

        return carry

    lax.fori_loop(0, 2 * shards, drain_out, 0)

    def collect(source, carry):
        for kind in range(4):
            for part in range(2):
                place = out_ref.at[kind, source, part_rows(part)]
                pltpu.make_async_copy(place, place, out_recv.at[kind, part, source]).wait()
        return carry

    lax.fori_loop(0, shards, collect, 0)


def rows_kernel(
    heads_ref, more_ref, out_a, out_b, out_c, out_d, held, more, wide, turned, in_sem, out_sem
):
    heads, rows, head_size = held.shape[1:]
    outs = (out_a, out_b, out_c, out_d)
    reads = [
        pltpu.make_async_copy(heads_ref.at[kind], held.at[kind], in_sem.at[kind])
        for kind in range(4)
    ]
    writes = [
        pltpu.make_async_copy(turned.at[kind], outs[kind], out_sem.at[kind]) for kind in range(4)
    ]
    half = more.shape[2]
    late = pltpu.make_async_copy(more_ref, more, in_sem.at[4])
    late.start()
    for read in reads:
        read.start()
    for kind in range(4):
        reads[kind].wait()
        if kind == DK:
            late.wait()
        for head in range(heads):
            wide[pl.ds(head, rows, stride=heads), :] = held[kind, head].astype(jnp.float32)
        if kind in (DK, DV):
            for slot in range(more.shape[1]):
                first = pl.ds((slot + heads // 2) % heads, half, stride=heads)
                wide[first, :] = wide[first, :] + more[kind - DK, slot].astype(jnp.float32)
        turned[kind] = wide[...].reshape(rows, heads, head_size).astype(jnp.bfloat16)
        writes[kind].start()
    for write in writes:
        write.wait()


def by_heads(queries, key_vecs, value_vecs, out_grad, doc_ids):
    shard_rows, head_count, head_size = queries.shape
    shards = lax.axis_size("ctx")
    half = shard_rows // 2
    tokens = shard_rows * shards
    group = 4
    size = group * half
    blocks = tokens // size
    slots = shards // 2 + shards // 4
    bf16, f32 = jnp.bfloat16, jnp.float32
    vmem = pl.BlockSpec(memory_space=pltpu.VMEM)
    flops = 7 * tokens * tokens * head_size
    results, more = pl.pallas_call(
        functools.partial(head_kernel, shards, half, group),
        out_shape=[
            jax.ShapeDtypeStruct((4, shards, shard_rows, head_size), bf16),
            jax.ShapeDtypeStruct((2, slots, half, head_size), bf16),
        ],
        in_specs=[pl.BlockSpec(memory_space=pltpu.HBM)] * 4 + [vmem],
        out_specs=[pl.BlockSpec(memory_space=pl.ANY)] * 2,
        scratch_shapes=[
            pltpu.VMEM((4, shard_rows, shards, head_size), bf16),
            pltpu.VMEM((4, shards, shard_rows, head_size), bf16),
            pltpu.VMEM((tokens, head_size), f32),
            pltpu.VMEM((4, tokens + 2 * size, head_size), bf16),
            pltpu.VMEM((4, tokens + 2 * size, head_size), bf16),
            pltpu.VMEM((2, shards // 2, half, head_size), bf16),
            pltpu.VMEM((blocks, size, 128), f32),
            pltpu.VMEM((blocks + 2, head_size, size), bf16),
            pltpu.VMEM((blocks + 2, head_size, size), bf16),
            pltpu.VMEM((blocks + 2, head_size, size), f32),
            pltpu.VMEM((blocks, size, size), f32),
            pltpu.VMEM((blocks + 2, blocks, size, size), bf16),
            pltpu.VMEM((blocks + 2, size, head_size), f32),
            pltpu.VMEM((blocks + 2, size, head_size), f32),
            pltpu.VMEM((blocks + 2, head_size, size), f32),
            pltpu.VMEM((blocks + 2, 1, size), f32),
            pltpu.SemaphoreType.DMA((4, 2, shards)),
            pltpu.SemaphoreType.DMA((4, 3 * shards)),
            pltpu.SemaphoreType.DMA((4, 2 * shards)),
            pltpu.SemaphoreType.DMA((4, 2, shards)),
            pltpu.SemaphoreType.DMA((4,)),
            pltpu.SemaphoreType.DMA((4, shards // 2)),
            pltpu.SemaphoreType.DMA((4, shards)),
            pltpu.SemaphoreType.DMA((2, slots)),
            pltpu.SemaphoreType.DMA((4, shards // 4)),
            pltpu.SemaphoreType.DMA,
        ],
        compiler_params=pltpu.CompilerParams(
            collective_id=0, has_side_effects=True, vmem_limit_bytes=VMEM_BYTES
        ),
        cost_estimate=pl.CostEstimate(
            flops=flops, bytes_accessed=8 * queries.size * 2, transcendentals=tokens * tokens // 2
        ),
    )(key_vecs, queries, value_vecs, out_grad, doc_ids)
    rows_first = jax.ShapeDtypeStruct((shard_rows, shards, head_size), bf16)
    return pl.pallas_call(
        rows_kernel,
        out_shape=[rows_first] * 4,
        in_specs=[pl.BlockSpec(memory_space=pl.ANY)] * 2,
        out_specs=[pl.BlockSpec(memory_space=pl.ANY)] * 4,
        scratch_shapes=[
            pltpu.VMEM((4, shards, shard_rows, head_size), bf16),
            pltpu.VMEM((2, slots, half, head_size), bf16),
            pltpu.VMEM((shard_rows * shards, head_size), f32),
            pltpu.VMEM((4, shard_rows, shards, head_size), bf16),
            pltpu.SemaphoreType.DMA((5,)),
            pltpu.SemaphoreType.DMA((4,)),
        ],
        compiler_params=pltpu.CompilerParams(vmem_limit_bytes=VMEM_BYTES),
        cost_estimate=pl.CostEstimate(
            flops=0, bytes_accessed=16 * queries.size, transcendentals=0
        ),
    )(results, more)


def on_device(queries, key_vecs, value_vecs, out_grad, doc_ids):
    shard_rows, head_count, head_size = queries.shape
    fits = (
        head_count == lax.axis_size("ctx")
        and head_count == 8
        and shard_rows % 32 == 0
        and (2 * shard_rows) % 128 == 0
        and head_size == 128
    )
    attend = by_heads if fits else gathered
    return attend(queries, key_vecs, value_vecs, out_grad, doc_ids)


def solution(mesh):
    return jax.shard_map(
        on_device,
        mesh=mesh,
        in_specs=(
            P(("grp", "ctx"), "head", None),
            P(("grp", "ctx"), "head", None),
            P(("grp", "ctx"), "head", None),
            P(("grp", "ctx"), "head", None),
            P("grp"),
        ),
        out_specs=(
            P(("grp", "ctx"), "head", None),
            P(("grp", "ctx"), "head", None),
            P(("grp", "ctx"), "head", None),
            P(("grp", "ctx"), "head", None),
        ),
        check_vma=False,
    )
```

```python
import functools

import jax
import jax.numpy as jnp
from jax import lax
from jax.experimental import pallas as pl
from jax.experimental.pallas import tpu as pltpu
from jax.sharding import PartitionSpec as P


def block_length(shard_rows, shard_count):
    factor = 1
    while factor * shard_rows < 512 and shard_count % (factor * 2) == 0:
        factor = factor * 2
    return factor * shard_rows


def stored_position(rows, shard_rows, shard_count):
    half_rows = shard_rows // 2
    shard = rows // shard_rows
    within = rows % shard_rows
    return jnp.where(
        within < half_rows,
        shard * half_rows + within,
        (2 * shard_count - 1 - shard) * half_rows + within - half_rows,
    )


def score_block(query_blk, query_pos, query_doc, key_blk, key_pos, key_doc, scaling):
    scores = (
        jnp.einsum("qhd,khd->hqk", query_blk, key_blk, preferred_element_type=jnp.float32) * scaling
    )
    allowed = (key_doc[None, :] == query_doc[:, None]) & (key_pos[None, :] <= query_pos[:, None])
    return (scores, allowed[None])


def probs_of(scores, allowed, lse):
    return jnp.where(allowed, jnp.exp(scores - lse[:, :, None]), 0.0).astype(jnp.bfloat16)


def dscores_of(probs, grad_blk, value_blk, delta):
    dprobs = jnp.einsum("qhd,khd->hqk", grad_blk, value_blk, preferred_element_type=jnp.float32)
    return (probs.astype(jnp.float32) * (dprobs - delta[:, :, None])).astype(jnp.bfloat16)


def gathered(queries, key_vecs, value_vecs, out_grad, doc_ids):
    shard_rows = queries.shape[0]
    head_count = queries.shape[1]
    head_size = queries.shape[2]
    scaling = head_size ** (-0.5)
    shard_count = lax.axis_size("ctx")
    shard_index = lax.axis_index("ctx")
    own_start = shard_index * shard_rows

    def positions(start, length):
        return stored_position(start + jnp.arange(length, dtype=jnp.int32), shard_rows, shard_count)

    own_pos = positions(own_start, shard_rows)
    own_doc = jnp.take(doc_ids, own_pos)
    keys_all, values_all = (
        lax.all_gather(key_vecs, "ctx", axis=0, tiled=True),
        lax.all_gather(value_vecs, "ctx", axis=0, tiled=True),
    )
    block = block_length(shard_rows, shard_count)
    block_count = keys_all.shape[0] // block

    def key_slices(start, length):
        key_blk = lax.dynamic_slice_in_dim(keys_all, start, length, 0)
        value_blk = lax.dynamic_slice_in_dim(values_all, start, length, 0)
        key_pos = positions(start, length)
        key_doc = jnp.take(doc_ids, key_pos)
        return (key_blk, value_blk, key_pos, key_doc)

    def stat_step(index, carry):
        running, total = carry
        key_blk, value_blk, key_pos, key_doc = key_slices(index * block, block)
        scores, allowed = score_block(queries, own_pos, own_doc, key_blk, key_pos, key_doc, scaling)
        newmax = jnp.maximum(running, jnp.max(jnp.where(allowed, scores, -1e30), axis=-1))
        total = total * jnp.exp(running - newmax) + jnp.sum(
            jnp.where(allowed, jnp.exp(scores - newmax[:, :, None]), 0.0), axis=-1
        )
        return (newmax, total)

    start_max = jnp.full((head_count, shard_rows), -1e30, jnp.float32)
    start_sum = jnp.zeros((head_count, shard_rows), jnp.float32)
    running, total = lax.fori_loop(0, block_count, stat_step, (start_max, start_sum))
    lse = running + jnp.log(total)

    def out_step(index, accum):
        key_blk, value_blk, key_pos, key_doc = key_slices(index * block, block)
        scores, allowed = score_block(queries, own_pos, own_doc, key_blk, key_pos, key_doc, scaling)
        probs = probs_of(scores, allowed, lse)
        return accum + jnp.einsum(
            "hqk,khd->qhd", probs, value_blk, preferred_element_type=jnp.float32
        )

    zero_rows = jnp.zeros((shard_rows, head_count, head_size), jnp.float32)
    attn_out = lax.fori_loop(0, block_count, out_step, zero_rows).astype(jnp.bfloat16)
    delta_rows = jnp.sum(out_grad.astype(jnp.float32) * attn_out.astype(jnp.float32), axis=-1)
    delta = delta_rows.T

    def query_step(index, accum):
        key_blk, value_blk, key_pos, key_doc = key_slices(index * block, block)
        scores, allowed = score_block(queries, own_pos, own_doc, key_blk, key_pos, key_doc, scaling)
        probs = probs_of(scores, allowed, lse)
        dscores = dscores_of(probs, out_grad, value_blk, delta)
        return accum + jnp.einsum(
            "hqk,khd->qhd", dscores, key_blk, preferred_element_type=jnp.float32
        )

    query_grad = (scaling * lax.fori_loop(0, block_count, query_step, zero_rows)).astype(
        jnp.bfloat16
    )
    lse_all, delta_all = (
        lax.all_gather(lse.T, "ctx", axis=0, tiled=True),
        lax.all_gather(delta_rows, "ctx", axis=0, tiled=True),
    )
    query_blk = lax.all_gather(queries, "ctx", axis=0, tiled=True)
    grad_blk = lax.all_gather(out_grad, "ctx", axis=0, tiled=True)
    length = query_blk.shape[0]
    query_pos = positions(jnp.int32(0), length)
    query_doc = jnp.take(doc_ids, query_pos)
    lse_blk = lse_all.T
    delta_blk = delta_all.T
    scores, allowed = score_block(
        query_blk, query_pos, query_doc, key_vecs, own_pos, own_doc, scaling
    )
    probs = probs_of(scores, allowed, lse_blk)
    dscores = dscores_of(probs, grad_blk, value_vecs, delta_blk)
    key_accum = scaling * jnp.einsum(
        "hqk,qhd->khd", dscores, query_blk, preferred_element_type=jnp.float32
    )
    value_accum = jnp.einsum("hqk,qhd->khd", probs, grad_blk, preferred_element_type=jnp.float32)
    key_grad = key_accum.astype(jnp.bfloat16)
    value_grad = value_accum.astype(jnp.bfloat16)
    return (attn_out, query_grad, key_grad, value_grad)


KEY, QUERY, VALUE, GRAD = 0, 1, 2, 3
OUT, DQ, DK, DV = 0, 1, 2, 3
VMEM_BYTES = 62 * 1024 * 1024 + 600 * 1024
LOG2E = 1.4426950408889634


def nt_dot(a, b):
    return lax.dot_general(a, b, (((1,), (1,)), ((), ())), preferred_element_type=jnp.float32)


def head_kernel(
    shards,
    half,
    group,
    key_ref,
    query_ref,
    value_ref,
    grad_ref,
    doc_ref,
    out_ref,
    more_ref,
    fetched,
    staged,
    wide,
    full,
    ready,
    zeros,
    doc_col,
    key_t,
    value_t,
    out_t,
    score_buf,
    prob_buf,
    key_acc,
    value_acc,
    query_acc,
    deltas,
    in_send,
    in_recv,
    out_send,
    out_recv,
    fetch_sem,
    low_send,
    more_send,
    more_recv,
    help_send,
    zero_sem,
):
    me = lax.axis_index("ctx")
    lower = shards // 2
    low = me < lower
    helpers = lower // 2
    helped = me < helpers
    helping = (me >= lower) & (me < lower + helpers)
    size = half * group
    blocks = 2 * shards // group
    head_size = full.shape[-1]
    scaling = head_size ** (-0.5)

    fetches = [
        pltpu.make_async_copy(ref, fetched.at[kind], fetch_sem.at[kind])
        for kind, ref in ((KEY, key_ref), (QUERY, query_ref), (VALUE, value_ref), (GRAD, grad_ref))
    ]
    for fetch in fetches:
        fetch.start()

    barrier = pltpu.get_barrier_semaphore()

    def greet(step, carry):
        pl.semaphore_signal(
            barrier,
            inc=1,
            device_id={"ctx": lax.rem(me + step, shards)},
            device_id_type=pl.DeviceIdType.MESH,
        )
        return carry

    lax.fori_loop(1, shards, greet, 0)

    def stage(kind):
        fetches[kind].wait()
        rows = fetched.shape[1]
        wide[...] = fetched[kind].astype(jnp.float32).reshape(rows * shards, head_size)
        for head in range(shards):
            staged[kind, head] = wide[pl.ds(head, rows, stride=shards), :].astype(jnp.bfloat16)

    def part_rows(part):
        return pl.ds(part * half, half)

    def block_rows(index):
        return pl.ds(pl.multiple_of(index * half, half), half)

    def position(part):
        return me if part == 0 else 2 * shards - 1 - me

    def far_first(step):
        return lax.rem(step + shards // 2 - 2, shards - 1) + 1

    def diverted(kind, part, target):
        if part == 1 or kind in (KEY, VALUE):
            return None
        return (low & (target >= lower)) | ((me >= lower) & (target < helpers))

    def unless(skip, act):
        if skip is None:
            act()
        else:
            pl.when(jnp.logical_not(skip))(act)

    def sent_in(kind, part):
        def one(step, carry):
            target = lax.rem(me + far_first(step), shards)

            def act():
                left = staged.at[kind, target, part_rows(part)]
                pltpu.make_async_copy(left, left, in_send.at[kind, part, step]).wait()

            unless(diverted(kind, part, target), act)
            return carry

        lax.fori_loop(1, shards, one, 0)

    def send_in(kind, part):
        where = position(part)
        pltpu.make_async_copy(
            staged.at[kind, me, part_rows(part)],
            full.at[kind, block_rows(where)],
            in_recv.at[kind, where],
        ).start()

        def one(step, carry):
            target = lax.rem(me + far_first(step), shards)

            def act():
                pltpu.make_async_remote_copy(
                    src_ref=staged.at[kind, target, part_rows(part)],
                    dst_ref=full.at[kind, block_rows(where)],
                    send_sem=in_send.at[kind, part, step],
                    recv_sem=in_recv.at[kind, where],
                    device_id={"ctx": target},
                    device_id_type=pl.DeviceIdType.MESH,
                ).start()

            unless(diverted(kind, part, target), act)
            return carry

        lax.fori_loop(1, shards, one, 0)

    def send_low(kind):
        where = 2 * shards + me

        @pl.when(low)
        def _():
            pltpu.make_async_copy(
                staged.at[kind, me + lower, part_rows(0)],
                full.at[kind, block_rows(where)],
                in_recv.at[kind, where],
            ).start()

            def one(step, carry):
                target = lax.rem(me + step, lower)
                pltpu.make_async_remote_copy(
                    src_ref=staged.at[kind, target + lower, part_rows(0)],
                    dst_ref=full.at[kind, block_rows(where)],
                    send_sem=low_send.at[kind, step],
                    recv_sem=in_recv.at[kind, where],
                    device_id={"ctx": target},
                    device_id_type=pl.DeviceIdType.MESH,
                ).start()
                return carry

            lax.fori_loop(1, lower, one, 0)

        for head in range(helpers):
            held = staged.at[kind, head, part_rows(0)]
            place = full.at[kind, block_rows(where)]

            def act():
                send_piece(
                    held, place, lower + head, help_send.at[kind, head], in_recv.at[kind, where]
                )

            unless(low if kind in (QUERY, GRAD) else None, act)

    def wait_in(kind, block):
        def one(index, carry):
            held = full.at[kind, block_rows(index)]
            pltpu.make_async_copy(held, held, in_recv.at[kind, index]).wait()
            return carry

        lax.fori_loop(block * group, (block + 1) * group, one, 0)

    def send_piece(held, place, owner, send_sem, recv_sem):
        @pl.when(owner == me)
        def _():
            pltpu.make_async_copy(held, place, recv_sem).start()

        @pl.when(owner != me)
        def _():
            pltpu.make_async_remote_copy(
                src_ref=held,
                dst_ref=place,
                send_sem=send_sem,
                recv_sem=recv_sem,
                device_id={"ctx": owner},
                device_id_type=pl.DeviceIdType.MESH,
            ).start()

    def send_out(kind, block):
        for index in range(block * group, (block + 1) * group):
            part = 0 if index < shards else 1
            owner = index if part == 0 else 2 * shards - 1 - index
            send_piece(
                ready.at[kind, pl.ds(index * half, half)],
                out_ref.at[kind, me, part_rows(part)],
                owner,
                out_send.at[kind, index],
                out_recv.at[kind, part, me],
            )

    def send_more(kind, block, head):
        for step in range(group):
            owner = (block - blocks) * group + step
            held = ready.at[kind, pl.ds((2 * shards + owner) * half, half)]
            if kind in (OUT, DQ):
                place = out_ref.at[kind, head, part_rows(0)]
                recv_sem = out_recv.at[kind, 0, head]
            else:
                place = more_ref.at[kind - DK, me]
                recv_sem = more_recv.at[kind - DK, me]
            send_piece(held, place, owner, more_send.at[kind, owner], recv_sem)

    stage(KEY)
    pl.semaphore_wait(barrier, shards - 1)
    send_in(KEY, 0)
    stage(QUERY)
    send_in(QUERY, 0)
    stage(VALUE)
    send_in(VALUE, 0)
    for kind in (KEY, QUERY, VALUE):
        send_low(kind)
    stage(GRAD)
    send_low(GRAD)

    docs = doc_ref[...].astype(jnp.float32).reshape(1, -1)
    for block in range(blocks):
        piece = docs[:, block * size : (block + 1) * size]
        doc_col[block] = jnp.broadcast_to(piece, (128, size)).T

    for kind in (KEY, QUERY, VALUE):
        sent_in(kind, 0)
        send_in(kind, 1)

    def rows_of(block):
        return pl.ds(block * size, size)

    def turn_keys(block):
        value_t[block] = full[VALUE, rows_of(block)].astype(jnp.float32).T.astype(jnp.bfloat16)
        key_t[block] = full[KEY, rows_of(block)].astype(jnp.float32).T.astype(jnp.bfloat16)

    def send_block(kind, block, head):
        if block >= blocks:
            send_more(kind, block, head)
        else:
            send_out(kind, block)

    def keys_of(block):
        return list(range(block, blocks - 1 if block >= blocks else -1, -1))

    def forward(block, head=None):
        keys = keys_of(block)
        for other in keys[1:]:
            if block >= blocks:
                wait_in(KEY, other)
                wait_in(VALUE, other)
                turn_keys(other)
        wait_in(KEY, block)
        wait_in(QUERY, block)
        queries = full[QUERY, rows_of(block)]
        at = block % blocks * size
        query_doc = docs[:, at : at + size]
        largest = None
        for other in keys:
            scores = nt_dot(full[KEY, rows_of(other)], queries)
            key_doc = jnp.concatenate([doc_col[other % blocks]] * (size // 128), axis=1)
            seen = key_doc == query_doc
            if other == block:
                key_at = lax.broadcasted_iota(jnp.int32, (size, size), 0)
                query_at = lax.broadcasted_iota(jnp.int32, (size, size), 1)
                seen = seen & (key_at <= query_at)
            scores = jnp.where(seen, scores, -1e30)
            score_buf[other % blocks] = scores
            top = jnp.max(scores, axis=0, keepdims=True)
            largest = top if largest is None else jnp.maximum(largest, top)
        total = jnp.zeros((1, size), jnp.float32)
        for other in keys:
            weights = jnp.exp2((score_buf[other % blocks] - largest) * (scaling * LOG2E))
            score_buf[other % blocks] = weights
            total = total + jnp.sum(weights, axis=0, keepdims=True)
        inverse = 1.0 / total
        wait_in(VALUE, block)
        turn_keys(block)
        accum = jnp.zeros((head_size, size), jnp.float32)
        for other in keys:
            probs = (score_buf[other % blocks] * inverse).astype(jnp.bfloat16)
            prob_buf[block, other % blocks] = probs
            accum = accum + jnp.dot(value_t[other], probs, preferred_element_type=jnp.float32)
        rounded = accum.astype(jnp.bfloat16).astype(jnp.float32)
        out_t[block] = rounded
        ready[OUT, rows_of(block)] = rounded.T.astype(jnp.bfloat16)
        send_block(OUT, block, head)

    def backward(pairs, new=(), done=(), head=None):
        for block, other in pairs:
            queries = full[QUERY, rows_of(block)]
            grads = full[GRAD, rows_of(block)]
            probs = prob_buf[block, other % blocks]
            dprobs = nt_dot(full[VALUE, rows_of(other)], grads)
            dscores = (probs.astype(jnp.float32) * (dprobs - deltas[block])).astype(jnp.bfloat16)
            value_part = jnp.dot(probs, grads, preferred_element_type=jnp.float32)
            key_part = jnp.dot(dscores, queries, preferred_element_type=jnp.float32)
            query_part = jnp.dot(key_t[other], dscores, preferred_element_type=jnp.float32)
            if ("k", block, other) not in new:
                value_part = value_part + value_acc[other]
                key_part = key_part + key_acc[other]
            if ("k", block, other) in done:
                finish_keys(other, value_part, key_part, head)
            else:
                value_acc[other] = value_part
                key_acc[other] = key_part
            if ("q", block, other) not in new:
                query_part = query_part + query_acc[block]
            if ("q", block, other) in done:
                ready[DQ, rows_of(block)] = (scaling * query_part).T.astype(jnp.bfloat16)
                send_block(DQ, block, head)
            else:
                query_acc[block] = query_part

    def ready_grads(block):
        wait_in(GRAD, block)
        grads = full[GRAD, rows_of(block)].astype(jnp.float32)
        deltas[block] = jnp.sum(grads.T * out_t[block], axis=0, keepdims=True)

    def plan(pairs):
        seen, new = set(), []
        for block, other in pairs:
            for name in (("q", block), ("k", other)):
                if name not in seen:
                    new.append((name[0], block, other))
                seen.add(name)
        return new

    def finish_keys(block, value_part, key_part, head=None):
        ready[DV, rows_of(block)] = value_part.astype(jnp.bfloat16)
        send_block(DV, block, head)
        ready[DK, rows_of(block)] = (scaling * key_part).astype(jnp.bfloat16)
        send_block(DK, block, head)

    def keys_alone(block):
        wait_in(KEY, block)
        wait_in(VALUE, block)
        turn_keys(block)

    def either(condition, first, second):
        pl.when(condition)(first)
        pl.when(jnp.logical_not(condition))(second)

    spare = more_ref.at[:, pl.ds(0, lower)]

    def fill_zeros():
        zeros[...] = jnp.zeros_like(zeros)
        pltpu.make_async_copy(zeros, spare, zero_sem).start()
        keys_alone(0)

    for kind, part in ((KEY, 1), (QUERY, 0)):
        sent_in(kind, 1)
        send_in(GRAD, part)

    either(low, lambda: forward(0), fill_zeros)
    either(helped, lambda: keys_alone(1), lambda: forward(1))

    @pl.when(low)
    def _():
        extra = blocks
        forward(extra, me + lower)
        ready_grads(extra)
        both = [("q", extra, extra), ("k", extra, extra)]
        backward([(extra, extra)], both, both, me + lower)

    @pl.when(helping)
    def _():
        extra = blocks + 1
        forward(extra, me - lower)
        ready_grads(extra)
        pairs = [(extra, blocks), (extra, extra)]
        done = [("k", extra, blocks), ("k", extra, extra), ("q", extra, extra)]
        backward(pairs, plan(pairs), done, me - lower)

    for block in range(2, blocks):
        forward(block)

    def lower_backward():
        late = blocks - 1
        first = [(late, late), (late, 2), (2, 2), (2, 1), (2, 0), (late, 1), (late, 0)]
        done = [("k", late, late), ("k", 2, 2), ("q", 2, 0), ("q", late, 0)]
        backward(first, plan(first), done)

        def second():
            ready_grads(1)
            backward([(1, 1), (1, 0)], [("q", 1, 1)], [("k", 1, 1), ("q", 1, 0)])

        either(helped, lambda: finish_keys(1, value_acc[1], key_acc[1]), second)
        ready_grads(0)
        backward([(0, 0)], [("q", 0, 0)], [("k", 0, 0), ("q", 0, 0)])

    def upper_backward():
        late = blocks - 1
        first = [(late, late), (late, 2), (2, 2), (late, 1), (late, 0), (2, 1), (2, 0)]
        done = [("k", late, late), ("k", 2, 2), ("q", late, 0), ("q", 2, 0)]
        backward(first, plan(first), done)
        ready_grads(1)
        done = [("k", 1, 0), ("k", 1, 1), ("q", 1, 1)]
        backward([(1, 0), (1, 1)], [("q", 1, 0)], done)
        pltpu.make_async_copy(zeros, spare, zero_sem).wait()

    for block in range(2, blocks):
        ready_grads(block)
    either(low, lower_backward, upper_backward)

    for kind, part in ((VALUE, 1), (GRAD, 1), (GRAD, 0)):
        sent_in(kind, part)

    @pl.when(low)
    def _():
        def drain_low(step, carry):
            for kind in range(4):
                left = staged.at[kind, lax.rem(me + step, lower) + lower, part_rows(0)]
                pltpu.make_async_copy(left, left, low_send.at[kind, step]).wait()
            return carry

        lax.fori_loop(1, lower, drain_low, 0)

        def drain_more(index, carry):
            @pl.when(index != me)
            def _():
                for kind in range(4):
                    left = ready.at[kind, block_rows(2 * shards + index)]
                    pltpu.make_async_copy(left, left, more_send.at[kind, index]).wait()

            return carry

        lax.fori_loop(0, lower, drain_more, 0)

    @pl.when(helping)
    def _():
        def drain_more(index, carry):
            @pl.when(index != me)
            def _():
                for kind in range(4):

                    def act():
                        left = ready.at[kind, block_rows(2 * shards + index)]
                        pltpu.make_async_copy(left, left, more_send.at[kind, index]).wait()

                    unless(index < lower if kind in (OUT, DQ) else None, act)

            return carry

        lax.fori_loop(0, shards, drain_more, 0)

    for head in range(helpers):

        @pl.when(me != lower + head)
        def _():
            for kind in range(4):

                def act():
                    left = staged.at[kind, head, part_rows(0)]
                    pltpu.make_async_copy(left, left, help_send.at[kind, head]).wait()

                unless(low if kind in (QUERY, GRAD) else None, act)

    def collect_more(source, carry):
        for kind in range(2):
            place = more_ref.at[kind, source]
            pltpu.make_async_copy(place, place, more_recv.at[kind, source]).wait()
        return carry

    @pl.when(low)
    def _():
        lax.fori_loop(0, lower, collect_more, 0)

    lax.fori_loop(lower, lower + helpers, collect_more, 0)

    def drain_out(index, carry):
        owner = jnp.where(index < shards, index, 2 * shards - 1 - index)

        @pl.when(owner != me)
        def _():
            for kind in range(4):

                def act():
                    left = ready.at[kind, block_rows(index)]
                    pltpu.make_async_copy(left, left, out_send.at[kind, index]).wait()

                kept = None
                if kind in (OUT, DQ):
                    kept = (jnp.logical_not(low) & (index < lower)) | (
                        helped & (index >= lower) & (index < shards)
                    )
                unless(kept, act)

        return carry

    lax.fori_loop(0, 2 * shards, drain_out, 0)

    def collect(source, carry):
        for kind in range(4):
            for part in range(2):
                place = out_ref.at[kind, source, part_rows(part)]
                pltpu.make_async_copy(place, place, out_recv.at[kind, part, source]).wait()
        return carry

    lax.fori_loop(0, shards, collect, 0)


def rows_kernel(
    heads_ref, more_ref, out_a, out_b, out_c, out_d, held, more, wide, turned, in_sem, out_sem
):
    heads, rows, head_size = held.shape[1:]
    outs = (out_a, out_b, out_c, out_d)
    reads = [
        pltpu.make_async_copy(heads_ref.at[kind], held.at[kind], in_sem.at[kind])
        for kind in range(4)
    ]
    writes = [
        pltpu.make_async_copy(turned.at[kind], outs[kind], out_sem.at[kind]) for kind in range(4)
    ]
    half = more.shape[2]
    late = pltpu.make_async_copy(more_ref, more, in_sem.at[4])
    late.start()
    for read in reads:
        read.start()
    for kind in range(4):
        reads[kind].wait()
        if kind == DK:
            late.wait()
        for head in range(heads):
            wide[pl.ds(head, rows, stride=heads), :] = held[kind, head].astype(jnp.float32)
        if kind in (DK, DV):
            for slot in range(more.shape[1]):
                first = pl.ds((slot + heads // 2) % heads, half, stride=heads)
                wide[first, :] = wide[first, :] + more[kind - DK, slot].astype(jnp.float32)
        turned[kind] = wide[...].reshape(rows, heads, head_size).astype(jnp.bfloat16)
        writes[kind].start()
    for write in writes:
        write.wait()


def by_heads(queries, key_vecs, value_vecs, out_grad, doc_ids):
    shard_rows, head_count, head_size = queries.shape
    shards = lax.axis_size("ctx")
    half = shard_rows // 2
    tokens = shard_rows * shards
    group = 4
    size = group * half
    blocks = tokens // size
    slots = shards // 2 + shards // 4
    bf16, f32 = jnp.bfloat16, jnp.float32
    vmem = pl.BlockSpec(memory_space=pltpu.VMEM)
    flops = 7 * tokens * tokens * head_size
    results, more = pl.pallas_call(
        functools.partial(head_kernel, shards, half, group),
        out_shape=[
            jax.ShapeDtypeStruct((4, shards, shard_rows, head_size), bf16),
            jax.ShapeDtypeStruct((2, slots, half, head_size), bf16),
        ],
        in_specs=[pl.BlockSpec(memory_space=pltpu.HBM)] * 4 + [vmem],
        out_specs=[pl.BlockSpec(memory_space=pl.ANY)] * 2,
        scratch_shapes=[
            pltpu.VMEM((4, shard_rows, shards, head_size), bf16),
            pltpu.VMEM((4, shards, shard_rows, head_size), bf16),
            pltpu.VMEM((tokens, head_size), f32),
            pltpu.VMEM((4, tokens + 2 * size, head_size), bf16),
            pltpu.VMEM((4, tokens + 2 * size, head_size), bf16),
            pltpu.VMEM((2, shards // 2, half, head_size), bf16),
            pltpu.VMEM((blocks, size, 128), f32),
            pltpu.VMEM((blocks + 2, head_size, size), bf16),
            pltpu.VMEM((blocks + 2, head_size, size), bf16),
            pltpu.VMEM((blocks + 2, head_size, size), f32),
            pltpu.VMEM((blocks, size, size), f32),
            pltpu.VMEM((blocks + 2, blocks, size, size), bf16),
            pltpu.VMEM((blocks + 2, size, head_size), f32),
            pltpu.VMEM((blocks + 2, size, head_size), f32),
            pltpu.VMEM((blocks + 2, head_size, size), f32),
            pltpu.VMEM((blocks + 2, 1, size), f32),
            pltpu.SemaphoreType.DMA((4, 2, shards)),
            pltpu.SemaphoreType.DMA((4, 3 * shards)),
            pltpu.SemaphoreType.DMA((4, 2 * shards)),
            pltpu.SemaphoreType.DMA((4, 2, shards)),
            pltpu.SemaphoreType.DMA((4,)),
            pltpu.SemaphoreType.DMA((4, shards // 2)),
            pltpu.SemaphoreType.DMA((4, shards)),
            pltpu.SemaphoreType.DMA((2, slots)),
            pltpu.SemaphoreType.DMA((4, shards // 4)),
            pltpu.SemaphoreType.DMA,
        ],
        compiler_params=pltpu.CompilerParams(
            collective_id=0, has_side_effects=True, vmem_limit_bytes=VMEM_BYTES
        ),
        cost_estimate=pl.CostEstimate(
            flops=flops, bytes_accessed=8 * queries.size * 2, transcendentals=tokens * tokens // 2
        ),
    )(key_vecs, queries, value_vecs, out_grad, doc_ids)
    rows_first = jax.ShapeDtypeStruct((shard_rows, shards, head_size), bf16)
    return pl.pallas_call(
        rows_kernel,
        out_shape=[rows_first] * 4,
        in_specs=[pl.BlockSpec(memory_space=pl.ANY)] * 2,
        out_specs=[pl.BlockSpec(memory_space=pl.ANY)] * 4,
        scratch_shapes=[
            pltpu.VMEM((4, shards, shard_rows, head_size), bf16),
            pltpu.VMEM((2, slots, half, head_size), bf16),
            pltpu.VMEM((shard_rows * shards, head_size), f32),
            pltpu.VMEM((4, shard_rows, shards, head_size), bf16),
            pltpu.SemaphoreType.DMA((5,)),
            pltpu.SemaphoreType.DMA((4,)),
        ],
        compiler_params=pltpu.CompilerParams(vmem_limit_bytes=VMEM_BYTES),
        cost_estimate=pl.CostEstimate(
            flops=0, bytes_accessed=16 * queries.size, transcendentals=0
        ),
    )(results, more)


def on_device(queries, key_vecs, value_vecs, out_grad, doc_ids):
    shard_rows, head_count, head_size = queries.shape
    fits = (
        head_count == lax.axis_size("ctx")
        and head_count == 8
        and shard_rows % 32 == 0
        and (2 * shard_rows) % 128 == 0
        and head_size == 128
    )
    attend = by_heads if fits else gathered
    return attend(queries, key_vecs, value_vecs, out_grad, doc_ids)


def solution(mesh):
    return jax.shard_map(
        on_device,
        mesh=mesh,
        in_specs=(
            P(("grp", "ctx"), "head", None),
            P(("grp", "ctx"), "head", None),
            P(("grp", "ctx"), "head", None),
            P(("grp", "ctx"), "head", None),
            P("grp"),
        ),
        out_specs=(
            P(("grp", "ctx"), "head", None),
            P(("grp", "ctx"), "head", None),
            P(("grp", "ctx"), "head", None),
            P(("grp", "ctx"), "head", None),
        ),
        check_vma=False,
    )
```
